32 devices in a mesh: dp: 4 (over x, core), ctx: 8 (over z, y).
Axes of the slice: x: 2, y: 2, z: 4, core: 2. Of those that a mesh axis runs over, the one named last changes fastest.
Arguments:
- queries: bfloat16 [4, 3072, 1536], P('dp', 'ctx'), may hold values from -160 to 160
- key_rows: bfloat16 [4, 3072, 1536], P('dp', 'ctx'), may hold values from -8 to 8
- value_rows: bfloat16 [4, 3072, 1536], P('dp', 'ctx'), may hold values from -6 to 6
- tile_lists: int32 [4, 8, 5], P('dp', 'ctx'), may hold values from 0 to 7, as said below
- tile_counts: int32 [4, 8], P('dp', 'ctx'), may hold values from 1 to 5
- out_weight: bfloat16 [1536, 1536], P('dp'), may hold values from -0.15625 to 0.15625
Outputs:
- projected: bfloat16 [4, 3072, 1536], P('dp', 'ctx')
The draws below stay inside these ranges and needn't reach their ends.
Inputs may be any that keep to these rules, and one draw needn't show every extreme that they name: For s < tile_counts[b, t], tile_lists[b, t, s] are distinct tiles of the video within 2 of t, increasing, and t is among them; later slots hold t.
All inputs are finite; a program needn't handle non-finite values.
Results may differ from the reference program's by a relative error of at most 0.0056.
Values may be sent and summed in bfloat16 or wider, within the bound.
A program may use at most 64 MiB of HBM per device.

```python
import math
import jax
import jax.numpy as jnp
from jax import lax

TILE = 384
HEADS = 12
HD = 128
DOUT = 1536
REACH = 2
SLOTS = 5
NT = 8
VIDEOS = 4
TOKENS = 3072


def window_plan(key):
    base_key = jax.random.fold_in(key, 7)
    bits = jax.random.randint(jax.random.fold_in(base_key, 1), (VIDEOS, NT, SLOTS), 0, 2)
    offsets = jnp.arange(SLOTS, dtype=jnp.int32)[None, None, :] - REACH
    tile_ids = jnp.arange(NT, dtype=jnp.int32)[None, :, None]
    targets = tile_ids + offsets
    full_tile = jax.random.randint(jax.random.fold_in(base_key, 2), (VIDEOS,), REACH, NT - REACH)
    lone_tile = jax.random.randint(jax.random.fold_in(base_key, 3), (VIDEOS,), 0, NT)
    lone_tile = jnp.where(lone_tile == full_tile, (full_tile + 1) % NT, lone_tile)
    chosen = jnp.where(tile_ids == full_tile[:, None, None], 1, bits)
    chosen = jnp.where(tile_ids == lone_tile[:, None, None], 0, chosen)
    chosen = jnp.where(offsets == 0, 1, chosen)
    chosen = jnp.where((targets >= 0) & (targets < NT), chosen, 0)
    order_keys = jnp.where(chosen == 1, offsets, offsets + 4 * SLOTS)
    order = jnp.argsort(order_keys, axis=-1, stable=True)
    sorted_offsets = jnp.take_along_axis(jnp.broadcast_to(offsets, chosen.shape), order, axis=-1)
    counted = jnp.sum(chosen, axis=-1)
    slot_ids = jnp.arange(SLOTS, dtype=jnp.int32)[None, None, :]
    lists = jnp.where(slot_ids < counted[..., None], tile_ids + sorted_offsets, tile_ids)
    return (lists.astype(jnp.int32), counted.astype(jnp.int32))


def draw_tile_lists(key, part):
    return window_plan(key)[0]


def draw_tile_counts(key, part):
    return window_plan(key)[1]


def shaped_keys(key):
    sampled = jax.random.normal(jax.random.fold_in(key, 23), (VIDEOS, TOKENS, HEADS, HD), jnp.float32)
    return jnp.clip(sampled, -8.0, 8.0)


def draw_key_rows(key, part):
    return shaped_keys(key).reshape(VIDEOS, TOKENS, HEADS * HD).astype(jnp.bfloat16)


def draw_queries(key, part):
    sampled = jax.random.normal(jax.random.fold_in(key, 31), (VIDEOS, TOKENS, HEADS, HD), jnp.float32)
    sampled = jnp.clip(sampled, -160.0, 160.0)
    return sampled.reshape(VIDEOS, TOKENS, HEADS * HD).astype(jnp.bfloat16)


def block_scale(rng, dims, pieces, least, high):
    gain, own = 1.0, jax.random.fold_in(rng, 6)
    for axis_at, shards_of in pieces:
        heights = jnp.exp(jax.random.uniform(jax.random.fold_in(own, axis_at), (shards_of,), jnp.float32, least / len(pieces), high / len(pieces)))
        gain = gain * jnp.repeat(heights, dims[axis_at] // shards_of).reshape([-1 if axis == axis_at else 1 for axis in range(len(dims))])
    return gain


def bell_draw(key, extent, scale, bound, pieces=(), kind=jnp.bfloat16):
    entries = jax.random.normal(key, extent, jnp.float32) * scale
    if len(pieces) > 0:
        entries = block_scale(key, extent, pieces, -0.22, 0.18) * entries
    return jnp.clip(entries, min=-bound, max=bound).astype(kind)


def setup_inputs(seed: int = 0) -> dict:
    splits = jax.random.split(jax.random.key(seed), 7)
    queries = draw_queries(jax.random.fold_in(splits[6], 71), 0)
    key_rows = draw_key_rows(jax.random.fold_in(splits[6], 71), 0)
    value_rows = bell_draw(splits[2], (VIDEOS, TOKENS, HEADS * HD), 1.0, 6.0, ((0, 4), (1, 8)))
    tile_lists = draw_tile_lists(jax.random.fold_in(splits[6], 71), 0)
    tile_counts = draw_tile_counts(jax.random.fold_in(splits[6], 71), 0)
    out_weight = bell_draw(splits[5], (HEADS * HD, DOUT), (HEADS * HD) ** -0.5, 0.15625, ((0, 4),))
    return {"queries": queries, "key_rows": key_rows, "value_rows": value_rows, "tile_lists": tile_lists, "tile_counts": tile_counts, "out_weight": out_weight}


def window_mask(tile_lists, tile_counts):
    tile_ids = jnp.arange(NT, dtype=jnp.int32)[None, :, None, None]
    offsets = jnp.arange(SLOTS, dtype=jnp.int32)[None, None, None, :] - REACH
    in_use = (jnp.arange(SLOTS, dtype=jnp.int32)[None, None, :] < tile_counts[:, :, None])[..., None]
    matches = (tile_lists[..., None] == tile_ids + offsets) & in_use
    return jnp.any(matches, axis=2).astype(jnp.int32)

def attend(query_tile, key_window, value_window, visible_tiles):
    query_heads = query_tile.reshape(TILE, HEADS, HD).astype(jnp.float32)
    key_heads = key_window.reshape(SLOTS * TILE, HEADS, HD).astype(jnp.float32)
    value_heads = value_window.reshape(SLOTS * TILE, HEADS, HD).astype(jnp.float32)
    scores = jnp.einsum('thd,khd->htk', query_heads, key_heads, precision=lax.Precision.HIGHEST) * (1.0 / math.sqrt(HD))
    expanded = (jnp.repeat(visible_tiles, TILE) > 0)[None, None, :]
    peak_rows = lax.optimization_barrier(jnp.max(jnp.where(expanded, scores, jnp.float32(-1e+30)), axis=-1, keepdims=True))
    exponent = jnp.where(expanded, jnp.exp(scores - peak_rows), jnp.float32(0.0))
    totals = lax.optimization_barrier(jnp.sum(exponent, axis=-1))
    probs = exponent.astype(jnp.bfloat16)
    mixture = jnp.einsum('htk,khd->htd', probs.astype(jnp.float32), value_heads, precision=lax.Precision.HIGHEST)
    result = (mixture / totals[..., None]).astype(jnp.bfloat16)
    return result.transpose(1, 0, 2).reshape(TILE, HEADS * HD)

def reference(queries, key_rows, value_rows, tile_lists, tile_counts, out_weight):
    visible = window_mask(tile_lists, tile_counts)
    padding = jnp.zeros((REACH * TILE, HEADS * HD), jnp.bfloat16)

    def one_video(video_pos):
        query_block = queries[video_pos]
        key_block = jnp.concatenate([padding, key_rows[video_pos], padding], axis=0)
        value_block = jnp.concatenate([padding, value_rows[video_pos], padding], axis=0)
        visible_video = visible[video_pos]

        def one_tile(tile_pos):
            query_tile = lax.dynamic_slice_in_dim(query_block, tile_pos * TILE, TILE, 0)
            key_window = lax.dynamic_slice_in_dim(key_block, tile_pos * TILE, SLOTS * TILE, 0)
            value_window = lax.dynamic_slice_in_dim(value_block, tile_pos * TILE, SLOTS * TILE, 0)
            return attend(query_tile, key_window, value_window, visible_video[tile_pos])
        return lax.map(one_tile, jnp.arange(NT, dtype=jnp.int32)).reshape(TOKENS, HEADS * HD)
    attention = lax.map(one_video, jnp.arange(VIDEOS, dtype=jnp.int32))
    result = jnp.dot(attention.reshape(VIDEOS * TOKENS, HEADS * HD), out_weight, preferred_element_type=jnp.float32)
    return result.astype(jnp.bfloat16).reshape(VIDEOS, TOKENS, DOUT)
```

```python
import functools
import math

import jax
import jax.numpy as jnp
from jax import lax
from jax.experimental import pallas as pl
from jax.experimental.pallas import tpu as pltpu
from jax.sharding import PartitionSpec as P

HD = 128
REACH = 2
SLOTS = 5
WINDOW = 6
HIDDEN = -1e30
SHUT = 1e30


def kernel(tiles, q_ref, k_ref, v_ref, vis_ref, out_ref,
           q_held, k_held, v_held, vis_held, done, stage,
           own_sem, vis_sem, pair_send, pair_recv, own_send, pass_send, z_recv, back_send, back_recv):
    half = q_held.shape[1]
    me = lax.axis_index("ctx")
    side = lax.rem(me, 2)
    pair = me + 1 - 2 * side
    has_up = me + 2 < tiles
    has_down = me >= 2
    up, down = me + 2, me - 2
    scale = math.log2(math.e) / math.sqrt(HD)

    def columns(ref, which, c):
        return ref.at[0, :, pl.ds(pl.multiple_of((which * half + c) * HD, HD), HD)]

    def remote(src, dst, send, recv, target):
        return pltpu.make_async_remote_copy(
            src_ref=src, dst_ref=dst, send_sem=send, recv_sem=recv,
            device_id={"ctx": target}, device_id_type=pl.DeviceIdType.MESH,
        )

    def to_pair(c):
        return [
            remote(columns(k_ref, 1 - side, c), k_held.at[2 + side, c], pair_send.at[0, c], pair_recv.at[0, c], pair),
            remote(columns(v_ref, 1 - side, c), v_held.at[2 + side, c], pair_send.at[1, c], pair_recv.at[1, c], pair),
            remote(columns(q_ref, 1 - side, c), q_held.at[side, c], pair_send.at[2, c], pair_recv.at[2, c], pair),
        ]

    def from_pair(c):
        other = 1 - side
        return [
            remote(columns(k_ref, side, c), k_held.at[2 + other, c], pair_send.at[0, c], pair_recv.at[0, c], pair),
            remote(columns(v_ref, side, c), v_held.at[2 + other, c], pair_send.at[1, c], pair_recv.at[1, c], pair),
            remote(columns(q_ref, side, c), q_held.at[other, c], pair_send.at[2, c], pair_recv.at[2, c], pair),
        ]

    def own_out(c, way):
        first, target = ((0, up), (4, down))[way]
        return [
            remote(columns(k_ref, side, c), k_held.at[first + side, c], own_send.at[way, 0, c], z_recv.at[way, 0, 0, c], target),
            remote(columns(v_ref, side, c), v_held.at[first + side, c], own_send.at[way, 1, c], z_recv.at[way, 0, 1, c], target),
        ]

    def pass_on(c, way):
        first, target = ((0, up), (4, down))[way]
        other = 1 - side
        return [
            remote(k_held.at[2 + other, c], k_held.at[first + other, c], pass_send.at[way, 0, c], z_recv.at[way, 1, 0, c], target),
            remote(v_held.at[2 + other, c], v_held.at[first + other, c], pass_send.at[way, 1, c], z_recv.at[way, 1, 1, c], target),
        ]

    def own_in(c):
        return [
            pltpu.make_async_copy(columns(q_ref, side, c), q_held.at[side, c], own_sem.at[0, c]),
            pltpu.make_async_copy(columns(k_ref, side, c), k_held.at[2 + side, c], own_sem.at[1, c]),
            pltpu.make_async_copy(columns(v_ref, side, c), v_held.at[2 + side, c], own_sem.at[2, c]),
        ]

    def back(c):
        return remote(stage.at[c], done.at[side * half + c], back_send.at[c], back_recv.at[c], pair)

    vis_in = pltpu.make_async_copy(vis_ref, vis_held.at[side], vis_sem.at[0])
    vis_out = remote(vis_ref, vis_held.at[side], vis_sem.at[1], vis_sem.at[2], pair)
    vis_got = remote(vis_ref, vis_held.at[1 - side], vis_sem.at[1], vis_sem.at[2], pair)

    barrier = pltpu.get_barrier_semaphore()

    def greet(target):
        pl.semaphore_signal(barrier, inc=1, device_id={"ctx": target}, device_id_type=pl.DeviceIdType.MESH)

    greet(pair)

    @pl.when(has_up)
    def _():
        greet(up)

    @pl.when(has_down)
    def _():
        greet(down)

    vis_in.start()

    @pl.loop(0, half)
    def _(c):
        for copy in own_in(c):
            copy.start()

    pl.semaphore_wait(barrier, 1 + has_up.astype(jnp.int32) + has_down.astype(jnp.int32))

    vis_out.start()

    @pl.loop(0, half)
    def _(c):
        for copy in to_pair(c):
            copy.start()

        @pl.when(has_up)
        def _():
            for copy in own_out(c, 0):
                copy.start()

        @pl.when(has_down)
        def _():
            for copy in own_out(c, 1):
                copy.start()

    @pl.when(jnp.logical_not(has_down))
    def _():
        k_held[0:2] = jnp.zeros((2,) + k_held.shape[1:], k_held.dtype)
        v_held[0:2] = jnp.zeros((2,) + v_held.shape[1:], v_held.dtype)

    @pl.when(jnp.logical_not(has_up))
    def _():
        k_held[4:6] = jnp.zeros((2,) + k_held.shape[1:], k_held.dtype)
        v_held[4:6] = jnp.zeros((2,) + v_held.shape[1:], v_held.dtype)

    def forward(c):
        for copy in from_pair(c):
            copy.wait_recv()

        @pl.when(has_up)
        def _():
            for copy in pass_on(c, 0):
                copy.start()

        @pl.when(has_down)
        def _():
            for copy in pass_on(c, 1):
                copy.start()

    def attend(c, j):
        q = q_held[j, c]
        seen = [vis_held[j, o : o + 1, :] > 0.0 for o in range(SLOTS)]
        scores, peak = [], None
        for o in range(SLOTS):
            s = lax.dot_general(q, k_held[j + o, c], (((1,), (1,)), ((), ())), preferred_element_type=jnp.float32)
            scores.append(s)
            top = s[:, :HD]
            for lane in range(HD, s.shape[1], HD):
                top = jnp.maximum(top, s[:, lane : lane + HD])
            top = jnp.where(seen[o], top, HIDDEN)
            peak = top if peak is None else jnp.maximum(peak, top)
        peak = jnp.max(peak, axis=1, keepdims=True) * scale
        total, mixture = None, None
        for o in range(SLOTS):
            shift = jnp.where(seen[o][:, :1], peak, SHUT)
            p = jnp.exp2(scores[o] * scale - shift)
            for lane in range(0, p.shape[1], HD):
                part = p[:, lane : lane + HD]
                total = part if total is None else total + part
            part = jnp.dot(p.astype(jnp.bfloat16), v_held[j + o, c], preferred_element_type=jnp.float32)
            mixture = part if mixture is None else mixture + part
        total = jnp.sum(total, axis=1, keepdims=True)
        return (mixture / total).astype(jnp.bfloat16)

    vis_in.wait()
    vis_got.wait_recv()
    forward(0)

    @pl.loop(0, half)
    def _(c):
        @pl.when(c + 1 < half)
        def _():
            forward(c + 1)

        for copy in own_in(c):
            copy.wait()

        @pl.when(has_down)
        def _():
            for copy in own_out(c, 0) + pass_on(c, 0):
                copy.wait_recv()

        @pl.when(has_up)
        def _():
            for copy in own_out(c, 1) + pass_on(c, 1):
                copy.wait_recv()

        stage[c] = attend(c, 1 - side)
        back(c).start()
        done[side * half + c] = attend(c, side)

    @pl.loop(0, half)
    def _(c):
        for copy in to_pair(c):
            copy.wait_send()

        @pl.when(has_up)
        def _():
            for copy in own_out(c, 0) + pass_on(c, 0):
                copy.wait_send()

        @pl.when(has_down)
        def _():
            for copy in own_out(c, 1) + pass_on(c, 1):
                copy.wait_send()

        back(c).wait()

    vis_out.wait_send()
    for h in range(2 * half):
        out_ref[0, :, h * HD : (h + 1) * HD] = done[h]


def per_device(queries, key_rows, value_rows, tile_lists, tile_counts, out_weight):
    tok_rows, channels = queries.shape[1], queries.shape[2]
    tiles = lax.axis_size("ctx")
    heads = channels // HD
    half = heads // 2
    tile_here = lax.axis_index("ctx")
    offsets = jnp.arange(SLOTS, dtype=jnp.int32) - REACH
    in_use = jnp.arange(SLOTS, dtype=jnp.int32) < tile_counts[0, 0]
    matches = (tile_lists[0, 0, :, None] == (tile_here + offsets)[None, :]) & in_use[:, None]
    visible = jnp.any(matches, axis=0).astype(jnp.float32)
    visible = jnp.broadcast_to(jnp.pad(visible, (0, 8 - SLOTS))[:, None], (8, HD))
    any_spec = pl.BlockSpec(memory_space=pl.ANY)
    held = pltpu.VMEM((WINDOW, half, tok_rows, HD), jnp.bfloat16)
    dma = pltpu.SemaphoreType.DMA
    pairs = 2 * tok_rows * SLOTS * tok_rows * half
    attention = pl.pallas_call(
        functools.partial(kernel, tiles),
        out_shape=jax.ShapeDtypeStruct(queries.shape, jnp.bfloat16),
        in_specs=[any_spec] * 4,
        out_specs=pl.BlockSpec(memory_space=pltpu.VMEM),
        scratch_shapes=[
            pltpu.VMEM((2, half, tok_rows, HD), jnp.bfloat16),
            held,
            held,
            pltpu.VMEM((2, 8, HD), jnp.float32),
            pltpu.VMEM((heads, tok_rows, HD), jnp.bfloat16),
            pltpu.VMEM((half, tok_rows, HD), jnp.bfloat16),
            dma((3, half)),
            dma((3,)),
            dma((3, half)),
            dma((3, half)),
            dma((2, 2, half)),
            dma((2, 2, half)),
            dma((2, 2, 2, half)),
            dma((half,)),
            dma((half,)),
        ],
        compiler_params=pltpu.CompilerParams(
            collective_id=0, has_side_effects=True, vmem_limit_bytes=44 * 1024 * 1024
        ),
        cost_estimate=pl.CostEstimate(
            flops=4 * pairs * HD, bytes_accessed=60_000_000, transcendentals=pairs
        ),
    )(queries, key_rows, value_rows, visible)
    gathered = lax.all_gather(out_weight, "dp", axis=0, tiled=True)
    projected = jnp.dot(attention[0], gathered, preferred_element_type=jnp.float32)
    return projected.astype(jnp.bfloat16)[None]


def solution(mesh):
    in_specs = (
        P("dp", "ctx", None),
        P("dp", "ctx", None),
        P("dp", "ctx", None),
        P("dp", "ctx", None),
        P("dp", "ctx"),
        P("dp", None),
    )
    out_specs = P("dp", "ctx", None)
    return jax.shard_map(
        per_device, mesh=mesh, in_specs=in_specs, out_specs=out_specs, check_vma=False
    )
```

```python
import functools
import math

import jax
import jax.numpy as jnp
from jax import lax
from jax.experimental import pallas as pl
from jax.experimental.pallas import tpu as pltpu
from jax.sharding import PartitionSpec as P

HD = 128
REACH = 2
SLOTS = 5
WINDOW = 6
HIDDEN = -1e30
SHUT = 1e30
BLOCK = 256


def kernel(tiles, shards, q_ref, k_ref, v_ref, vis_ref, w_ref, out_ref,
           q_held, k_held, v_held, vis_held, done, stage, w_held,
           w_own, w_send, w_recv, w_pass, w_core, own_sem, vis_sem, pair_send, pair_recv, own_send, pass_send, z_recv, back_send, back_recv):
    half = q_held.shape[1]
    me = lax.axis_index("ctx")
    row = lax.axis_index("dp")
    sibling = row + 1 - 2 * lax.rem(row, 2)
    depth = w_ref.shape[0]
    chips = shards // 2
    side = lax.rem(me, 2)
    pair = me + 1 - 2 * side
    has_up = me + 2 < tiles
    has_down = me >= 2
    up, down = me + 2, me - 2
    scale = math.log2(math.e) / math.sqrt(HD)

    def columns(ref, which, c):
        return ref.at[0, :, pl.ds(pl.multiple_of((which * half + c) * HD, HD), HD)]

    def remote(src, dst, send, recv, target):
        return pltpu.make_async_remote_copy(
            src_ref=src, dst_ref=dst, send_sem=send, recv_sem=recv,
            device_id={"ctx": target}, device_id_type=pl.DeviceIdType.MESH,
        )

    def to_pair(c):
        return [
            remote(columns(k_ref, 1 - side, c), k_held.at[2 + side, c], pair_send.at[0, c], pair_recv.at[0, c], pair),
            remote(columns(v_ref, 1 - side, c), v_held.at[2 + side, c], pair_send.at[1, c], pair_recv.at[1, c], pair),
            remote(columns(q_ref, 1 - side, c), q_held.at[side, c], pair_send.at[2, c], pair_recv.at[2, c], pair),
        ]

    def from_pair(c):
        other = 1 - side
        return [
            remote(columns(k_ref, side, c), k_held.at[2 + other, c], pair_send.at[0, c], pair_recv.at[0, c], pair),
            remote(columns(v_ref, side, c), v_held.at[2 + other, c], pair_send.at[1, c], pair_recv.at[1, c], pair),
            remote(columns(q_ref, side, c), q_held.at[other, c], pair_send.at[2, c], pair_recv.at[2, c], pair),
        ]

    def own_out(c, way):
        first, target = ((0, up), (4, down))[way]
        return [
            remote(columns(k_ref, side, c), k_held.at[first + side, c], own_send.at[way, 0, c], z_recv.at[way, 0, 0, c], target),
            remote(columns(v_ref, side, c), v_held.at[first + side, c], own_send.at[way, 1, c], z_recv.at[way, 0, 1, c], target),
        ]

    def pass_on(c, way):
        first, target = ((0, up), (4, down))[way]
        other = 1 - side
        return [
            remote(k_held.at[2 + other, c], k_held.at[first + other, c], pass_send.at[way, 0, c], z_recv.at[way, 1, 0, c], target),
            remote(v_held.at[2 + other, c], v_held.at[first + other, c], pass_send.at[way, 1, c], z_recv.at[way, 1, 1, c], target),
        ]

    def own_in(c):
        return [
            pltpu.make_async_copy(columns(q_ref, side, c), q_held.at[side, c], own_sem.at[0, c]),
            pltpu.make_async_copy(columns(k_ref, side, c), k_held.at[2 + side, c], own_sem.at[1, c]),
            pltpu.make_async_copy(columns(v_ref, side, c), v_held.at[2 + side, c], own_sem.at[2, c]),
        ]

    def head(which, c):
        return done.at[:, pl.ds(pl.multiple_of((which * half + c) * HD, HD), HD)]

    def back(c):
        return remote(stage.at[c], head(side, c), back_send.at[c], back_recv.at[c], pair)

    def shard(owner):
        return w_held.at[pl.ds(pl.multiple_of(owner * depth, depth), depth)]

    def w_copy(src, owner, send, recv, target):
        return pltpu.make_async_remote_copy(
            src_ref=src, dst_ref=shard(owner), send_sem=send, recv_sem=recv,
            device_id={"dp": target}, device_id_type=pl.DeviceIdType.MESH,
        )

    def w_chip(k):
        return w_copy(w_ref, row, w_send.at[k], w_recv.at[k], lax.rem(row + 2 * k, shards))

    def w_from(k):
        return lax.rem(row + shards - 2 * k, shards)

    def w_sibling(k):
        src = w_ref if k == 0 else shard(w_from(k))
        return w_copy(src, w_from(k), w_pass.at[k], w_core.at[k], sibling)

    w_in = pltpu.make_async_copy(w_ref, shard(row), w_own.at[0])

    vis_in = pltpu.make_async_copy(vis_ref, vis_held.at[side], vis_sem.at[0])
    vis_out = remote(vis_ref, vis_held.at[side], vis_sem.at[1], vis_sem.at[2], pair)
    vis_got = remote(vis_ref, vis_held.at[1 - side], vis_sem.at[1], vis_sem.at[2], pair)

    barrier = pltpu.get_barrier_semaphore()

    def greet(target):
        pl.semaphore_signal(barrier, inc=1, device_id={"ctx": target}, device_id_type=pl.DeviceIdType.MESH)

    def greet_row(target):
        pl.semaphore_signal(barrier, inc=1, device_id={"dp": target}, device_id_type=pl.DeviceIdType.MESH)

    greet(pair)
    greet_row(sibling)
    for k in range(1, chips):
        greet_row(lax.rem(row + 2 * k, shards))

    @pl.when(has_up)
    def _():
        greet(up)

    @pl.when(has_down)
    def _():
        greet(down)

    vis_in.start()

    @pl.loop(0, half)
    def _(c):
        for copy in own_in(c):
            copy.start()

    pl.semaphore_wait(barrier, 1 + chips + has_up.astype(jnp.int32) + has_down.astype(jnp.int32))

    vis_out.start()

    @pl.loop(0, half)
    def _(c):
        for copy in to_pair(c):
            copy.start()

        @pl.when(has_up)
        def _():
            for copy in own_out(c, 0):
                copy.start()

        @pl.when(has_down)
        def _():
            for copy in own_out(c, 1):
                copy.start()

    w_in.start()
    for k in range(1, chips):
        w_chip(k).start()
    w_sibling(0).start()

    @pl.when(jnp.logical_not(has_down))
    def _():
        k_held[0:2] = jnp.zeros((2,) + k_held.shape[1:], k_held.dtype)
        v_held[0:2] = jnp.zeros((2,) + v_held.shape[1:], v_held.dtype)

    @pl.when(jnp.logical_not(has_up))
    def _():
        k_held[4:6] = jnp.zeros((2,) + k_held.shape[1:], k_held.dtype)
        v_held[4:6] = jnp.zeros((2,) + v_held.shape[1:], v_held.dtype)

    def forward(c):
        for copy in from_pair(c):
            copy.wait_recv()

        @pl.when(has_up)
        def _():
            for copy in pass_on(c, 0):
                copy.start()

        @pl.when(has_down)
        def _():
            for copy in pass_on(c, 1):
                copy.start()

    def attend(c, j):
        q = q_held[j, c]
        seen = [vis_held[j, o : o + 1, :] > 0.0 for o in range(SLOTS)]
        scores, peak = [], None
        for o in range(SLOTS):
            s = lax.dot_general(q, k_held[j + o, c], (((1,), (1,)), ((), ())), preferred_element_type=jnp.float32)
            scores.append(s)
            top = s[:, :HD]
            for lane in range(HD, s.shape[1], HD):
                top = jnp.maximum(top, s[:, lane : lane + HD])
            top = jnp.where(seen[o], top, HIDDEN)
            peak = top if peak is None else jnp.maximum(peak, top)
        peak = jnp.max(peak, axis=1, keepdims=True) * scale
        total, mixture = None, None
        for o in range(SLOTS):
            shift = jnp.where(seen[o][:, :1], peak, SHUT)
            p = jnp.exp2(scores[o] * scale - shift)
            for lane in range(0, p.shape[1], HD):
                part = p[:, lane : lane + HD]
                total = part if total is None else total + part
            part = jnp.dot(p.astype(jnp.bfloat16), v_held[j + o, c], preferred_element_type=jnp.float32)
            mixture = part if mixture is None else mixture + part
        total = jnp.sum(total, axis=1, keepdims=True)
        return (mixture / total).astype(jnp.bfloat16)

    vis_in.wait()
    vis_got.wait_recv()
    forward(0)

    @pl.loop(0, half)
    def _(c):
        @pl.when(c + 1 < half)
        def _():
            forward(c + 1)

        for copy in own_in(c):
            copy.wait()

        @pl.when(has_down)
        def _():
            for copy in own_out(c, 0) + pass_on(c, 0):
                copy.wait_recv()

        @pl.when(has_up)
        def _():
            for copy in own_out(c, 1) + pass_on(c, 1):
                copy.wait_recv()

        stage[c] = attend(c, 1 - side)
        back(c).start()
        head(side, c)[...] = attend(c, side)

        @pl.when(c == half // 2)
        def _():
            for k in range(1, chips):
                w_chip(k).wait_recv()
                w_sibling(k).start()

    @pl.loop(0, half)
    def _(c):
        for copy in to_pair(c):
            copy.wait_send()

        @pl.when(has_up)
        def _():
            for copy in own_out(c, 0) + pass_on(c, 0):
                copy.wait_send()

        @pl.when(has_down)
        def _():
            for copy in own_out(c, 1) + pass_on(c, 1):
                copy.wait_send()

        back(c).wait()

    vis_out.wait_send()
    w_in.wait()
    for k in range(1, chips):
        w_chip(k).wait_send()
    for k in range(chips):
        w_sibling(k).wait()

    @pl.loop(0, out_ref.shape[2] // BLOCK)
    def _(n):
        cols = pl.ds(pl.multiple_of(n * BLOCK, BLOCK), BLOCK)
        product = jnp.dot(done[...], w_held[:, cols], preferred_element_type=jnp.float32)
        out_ref[0, :, cols] = product.astype(jnp.bfloat16)


def per_device(queries, key_rows, value_rows, tile_lists, tile_counts, out_weight):
    tok_rows, channels = queries.shape[1], queries.shape[2]
    tiles = lax.axis_size("ctx")
    heads = channels // HD
    half = heads // 2
    tile_here = lax.axis_index("ctx")
    offsets = jnp.arange(SLOTS, dtype=jnp.int32) - REACH
    in_use = jnp.arange(SLOTS, dtype=jnp.int32) < tile_counts[0, 0]
    matches = (tile_lists[0, 0, :, None] == (tile_here + offsets)[None, :]) & in_use[:, None]
    visible = jnp.any(matches, axis=0).astype(jnp.float32)
    visible = jnp.broadcast_to(jnp.pad(visible, (0, 8 - SLOTS))[:, None], (8, HD))
    any_spec = pl.BlockSpec(memory_space=pl.ANY)
    held = pltpu.VMEM((WINDOW, half, tok_rows, HD), jnp.bfloat16)
    dma = pltpu.SemaphoreType.DMA
    pairs = 2 * tok_rows * SLOTS * tok_rows * half
    shards = lax.axis_size("dp")
    chips = shards // 2
    return pl.pallas_call(
        functools.partial(kernel, tiles, shards),
        out_shape=jax.ShapeDtypeStruct((1, tok_rows, out_weight.shape[1]), jnp.bfloat16),
        in_specs=[any_spec] * 5,
        out_specs=pl.BlockSpec(memory_space=pltpu.VMEM),
        scratch_shapes=[
            pltpu.VMEM((2, half, tok_rows, HD), jnp.bfloat16),
            held,
            held,
            pltpu.VMEM((2, 8, HD), jnp.float32),
            pltpu.VMEM((tok_rows, channels), jnp.bfloat16),
            pltpu.VMEM((half, tok_rows, HD), jnp.bfloat16),
            pltpu.VMEM((channels, out_weight.shape[1]), jnp.bfloat16),
            dma((1,)),
            dma((chips,)),
            dma((chips,)),
            dma((chips,)),
            dma((chips,)),
            dma((3, half)),
            dma((3,)),
            dma((3, half)),
            dma((3, half)),
            dma((2, 2, half)),
            dma((2, 2, half)),
            dma((2, 2, 2, half)),
            dma((half,)),
            dma((half,)),
        ],
        compiler_params=pltpu.CompilerParams(
            collective_id=0, has_side_effects=True, vmem_limit_bytes=60 * 1024 * 1024
        ),
        cost_estimate=pl.CostEstimate(
            flops=4 * pairs * HD, bytes_accessed=60_000_000, transcendentals=pairs
        ),
    )(queries, key_rows, value_rows, visible, out_weight)


def solution(mesh):
    in_specs = (
        P("dp", "ctx", None),
        P("dp", "ctx", None),
        P("dp", "ctx", None),
        P("dp", "ctx", None),
        P("dp", "ctx"),
        P("dp", None),
    )
    out_specs = P("dp", "ctx", None)
    return jax.shard_map(
        per_device, mesh=mesh, in_specs=in_specs, out_specs=out_specs, check_vma=False
    )
```

```python
import functools
import math

import jax
import jax.numpy as jnp
from jax import lax
from jax.experimental import pallas as pl
from jax.experimental.pallas import tpu as pltpu
from jax.sharding import PartitionSpec as P

HD = 128
REACH = 2
SLOTS = 5
WINDOW = 6
HIDDEN = -1e30
SHUT = 1e30
BLOCK = 256


def kernel(tiles, shards, q_ref, k_ref, v_ref, lists_ref, counts_ref, w_ref, out_ref,
           lists_held, counts_held, vis_mine, q_held, k_held, v_held, vis_held, done, stage, w_held,
           w_own, w_send, w_recv, w_pass, w_core, own_sem, vis_sem, pair_send, pair_recv, own_send, pass_send, z_recv, back_send, back_recv):
    half = q_held.shape[1]
    me = lax.axis_index("ctx")
    row = lax.axis_index("dp")
    sibling = row + 1 - 2 * lax.rem(row, 2)
    depth = w_ref.shape[0]
    chips = shards // 2
    side = lax.rem(me, 2)
    pair = me + 1 - 2 * side
    has_up = me + 2 < tiles
    has_down = me >= 2
    up, down = me + 2, me - 2
    scale = math.log2(math.e) / math.sqrt(HD)

    def columns(ref, which, c):
        return ref.at[0, :, pl.ds(pl.multiple_of((which * half + c) * HD, HD), HD)]

    def remote(src, dst, send, recv, target):
        return pltpu.make_async_remote_copy(
            src_ref=src, dst_ref=dst, send_sem=send, recv_sem=recv,
            device_id={"ctx": target}, device_id_type=pl.DeviceIdType.MESH,
        )

    def to_pair(c):
        return [
            remote(columns(k_ref, 1 - side, c), k_held.at[2 + side, c], pair_send.at[0, c], pair_recv.at[0, c], pair),
            remote(columns(v_ref, 1 - side, c), v_held.at[2 + side, c], pair_send.at[1, c], pair_recv.at[1, c], pair),
            remote(columns(q_ref, 1 - side, c), q_held.at[side, c], pair_send.at[2, c], pair_recv.at[2, c], pair),
        ]

    def from_pair(c):
        other = 1 - side
        return [
            remote(columns(k_ref, side, c), k_held.at[2 + other, c], pair_send.at[0, c], pair_recv.at[0, c], pair),
            remote(columns(v_ref, side, c), v_held.at[2 + other, c], pair_send.at[1, c], pair_recv.at[1, c], pair),
            remote(columns(q_ref, side, c), q_held.at[other, c], pair_send.at[2, c], pair_recv.at[2, c], pair),
        ]

    def own_out(c, way):
        first, target = ((0, up), (4, down))[way]
        return [
            remote(columns(k_ref, side, c), k_held.at[first + side, c], own_send.at[way, 0, c], z_recv.at[way, 0, 0, c], target),
            remote(columns(v_ref, side, c), v_held.at[first + side, c], own_send.at[way, 1, c], z_recv.at[way, 0, 1, c], target),
        ]

    def pass_on(c, way):
        first, target = ((0, up), (4, down))[way]
        other = 1 - side
        return [
            remote(k_held.at[2 + other, c], k_held.at[first + other, c], pass_send.at[way, 0, c], z_recv.at[way, 1, 0, c], target),
            remote(v_held.at[2 + other, c], v_held.at[first + other, c], pass_send.at[way, 1, c], z_recv.at[way, 1, 1, c], target),
        ]

    def own_in(c):
        return [
            pltpu.make_async_copy(columns(q_ref, side, c), q_held.at[side, c], own_sem.at[0, c]),
            pltpu.make_async_copy(columns(k_ref, side, c), k_held.at[2 + side, c], own_sem.at[1, c]),
            pltpu.make_async_copy(columns(v_ref, side, c), v_held.at[2 + side, c], own_sem.at[2, c]),
        ]

    def head(which, c):
        return done.at[:, pl.ds(pl.multiple_of((which * half + c) * HD, HD), HD)]

    def back(c):
        return remote(stage.at[c], head(side, c), back_send.at[c], back_recv.at[c], pair)

    def shard(owner):
        return w_held.at[pl.ds(pl.multiple_of(owner * depth, depth), depth)]

    def w_copy(src, owner, send, recv, target):
        return pltpu.make_async_remote_copy(
            src_ref=src, dst_ref=shard(owner), send_sem=send, recv_sem=recv,
            device_id={"dp": target}, device_id_type=pl.DeviceIdType.MESH,
        )

    def w_chip(k):
        return w_copy(w_ref, row, w_send.at[k], w_recv.at[k], lax.rem(row + 2 * k, shards))

    def w_from(k):
        return lax.rem(row + shards - 2 * k, shards)

    def w_sibling(k):
        src = w_ref if k == 0 else shard(w_from(k))
        return w_copy(src, w_from(k), w_pass.at[k], w_core.at[k], sibling)

    w_in = pltpu.make_async_copy(w_ref, shard(row), w_own.at[0])

    lists_in = pltpu.make_async_copy(lists_ref, lists_held, vis_sem.at[0])
    counts_in = pltpu.make_async_copy(counts_ref, counts_held, vis_sem.at[3])
    vis_out = remote(vis_mine, vis_held.at[side], vis_sem.at[1], vis_sem.at[2], pair)
    vis_got = remote(vis_mine, vis_held.at[1 - side], vis_sem.at[1], vis_sem.at[2], pair)

    barrier = pltpu.get_barrier_semaphore()

    def greet(target):
        pl.semaphore_signal(barrier, inc=1, device_id={"ctx": target}, device_id_type=pl.DeviceIdType.MESH)

    def greet_row(target):
        pl.semaphore_signal(barrier, inc=1, device_id={"dp": target}, device_id_type=pl.DeviceIdType.MESH)

    greet(pair)
    greet_row(sibling)
    for k in range(1, chips):
        greet_row(lax.rem(row + 2 * k, shards))

    @pl.when(has_up)
    def _():
        greet(up)

    @pl.when(has_down)
    def _():
        greet(down)

    lists_in.start()
    counts_in.start()

    @pl.loop(0, half)
    def _(c):
        for copy in own_in(c):
            copy.start()

    pl.semaphore_wait(barrier, 1 + chips + has_up.astype(jnp.int32) + has_down.astype(jnp.int32))

    @pl.loop(0, half)
    def _(c):
        for copy in to_pair(c)[:2]:
            copy.start()

        @pl.when(has_up)
        def _():
            for copy in own_out(c, 0):
                copy.start()

        @pl.when(has_down)
        def _():
            for copy in own_out(c, 1):
                copy.start()

    w_in.start()
    for k in range(1, chips):
        w_chip(k).start()
    w_sibling(0).start()

    lists_in.wait()
    counts_in.wait()
    listed = lists_held[0]
    live = lax.broadcasted_iota(jnp.int32, listed.shape, 1) < counts_held[...]
    for o in range(SLOTS):
        match = jnp.where((listed == me + (o - REACH)) & live, 1.0, 0.0)
        row_seen = jnp.max(match, axis=1, keepdims=True)
        vis_mine[o : o + 1, :] = jnp.broadcast_to(row_seen, (1, HD))
        vis_held[side, o : o + 1, :] = jnp.broadcast_to(row_seen, (1, HD))
    vis_out.start()

    @pl.when(jnp.logical_not(has_down))
    def _():
        k_held[0:2] = jnp.zeros((2,) + k_held.shape[1:], k_held.dtype)
        v_held[0:2] = jnp.zeros((2,) + v_held.shape[1:], v_held.dtype)

    @pl.when(jnp.logical_not(has_up))
    def _():
        k_held[4:6] = jnp.zeros((2,) + k_held.shape[1:], k_held.dtype)
        v_held[4:6] = jnp.zeros((2,) + v_held.shape[1:], v_held.dtype)

    @pl.loop(0, half)
    def _(c):
        for copy in from_pair(c)[:2]:
            copy.wait_recv()
        to_pair(c)[2].start()

        @pl.when(has_up)
        def _():
            for copy in pass_on(c, 0):
                copy.start()

        @pl.when(has_down)
        def _():
            for copy in pass_on(c, 1):
                copy.start()

    def attend(c, j):
        q = q_held[j, c]
        seen = [vis_held[j, o : o + 1, :] > 0.0 for o in range(SLOTS)]
        scores, peak = [], None
        for o in range(SLOTS):
            s = lax.dot_general(q, k_held[j + o, c], (((1,), (1,)), ((), ())), preferred_element_type=jnp.float32)
            scores.append(s)
            top = s[:, :HD]
            for lane in range(HD, s.shape[1], HD):
                top = jnp.maximum(top, s[:, lane : lane + HD])
            top = jnp.where(seen[o], top, HIDDEN)
            peak = top if peak is None else jnp.maximum(peak, top)
        peak = jnp.max(peak, axis=1, keepdims=True) * scale
        total, mixture = None, None
        for o in range(SLOTS):
            shift = jnp.where(seen[o][:, :1], peak, SHUT)
            p = jnp.exp2(scores[o] * scale - shift)
            for lane in range(0, p.shape[1], HD):
                part = p[:, lane : lane + HD]
                total = part if total is None else total + part
            part = jnp.dot(p.astype(jnp.bfloat16), v_held[j + o, c], preferred_element_type=jnp.float32)
            mixture = part if mixture is None else mixture + part
        total = jnp.sum(total, axis=1, keepdims=True)
        return (mixture / total).astype(jnp.bfloat16)

    vis_got.wait_recv()

    @pl.loop(0, half)
    def _(c):
        for copy in own_in(c):
            copy.wait()
        from_pair(c)[2].wait_recv()

        @pl.when(has_down)
        def _():
            for copy in own_out(c, 0) + pass_on(c, 0):
                copy.wait_recv()

        @pl.when(has_up)
        def _():
            for copy in own_out(c, 1) + pass_on(c, 1):
                copy.wait_recv()

        stage[c] = attend(c, 1 - side)
        back(c).start()
        head(side, c)[...] = attend(c, side)

        @pl.when(c == half // 2)
        def _():
            for k in range(1, chips):
                w_chip(k).wait_recv()
                w_sibling(k).start()

    @pl.loop(0, half)
    def _(c):
        for copy in to_pair(c):
            copy.wait_send()

        @pl.when(has_up)
        def _():
            for copy in own_out(c, 0) + pass_on(c, 0):
                copy.wait_send()

        @pl.when(has_down)
        def _():
            for copy in own_out(c, 1) + pass_on(c, 1):
                copy.wait_send()

        back(c).wait()

    vis_out.wait_send()
    w_in.wait()
    for k in range(1, chips):
        w_chip(k).wait_send()
    for k in range(chips):
        w_sibling(k).wait()

    @pl.loop(0, out_ref.shape[2] // BLOCK)
    def _(n):
        cols = pl.ds(pl.multiple_of(n * BLOCK, BLOCK), BLOCK)
        product = jnp.dot(done[...], w_held[:, cols], preferred_element_type=jnp.float32)
        out_ref[0, :, cols] = product.astype(jnp.bfloat16)


def per_device(queries, key_rows, value_rows, tile_lists, tile_counts, out_weight):
    tok_rows, channels = queries.shape[1], queries.shape[2]
    tiles = lax.axis_size("ctx")
    heads = channels // HD
    half = heads // 2
    hbm_spec = pl.BlockSpec(memory_space=pltpu.HBM)
    held = pltpu.VMEM((WINDOW, half, tok_rows, HD), jnp.bfloat16)
    dma = pltpu.SemaphoreType.DMA
    pairs = 2 * tok_rows * SLOTS * tok_rows * half
    shards = lax.axis_size("dp")
    chips = shards // 2
    return pl.pallas_call(
        functools.partial(kernel, tiles, shards),
        out_shape=pltpu.VMEM((1, tok_rows, out_weight.shape[1]), jnp.bfloat16),
        in_specs=[hbm_spec] * 6,
        out_specs=pl.BlockSpec(memory_space=pltpu.VMEM),
        scratch_shapes=[
            pltpu.VMEM(tile_lists.shape, jnp.int32),
            pltpu.VMEM(tile_counts.shape, jnp.int32),
            pltpu.VMEM((8, HD), jnp.float32),
            pltpu.VMEM((2, half, tok_rows, HD), jnp.bfloat16),
            held,
            held,
            pltpu.VMEM((2, 8, HD), jnp.float32),
            pltpu.VMEM((tok_rows, channels), jnp.bfloat16),
            pltpu.VMEM((half, tok_rows, HD), jnp.bfloat16),
            pltpu.VMEM((channels, out_weight.shape[1]), jnp.bfloat16),
            dma((1,)),
            dma((chips,)),
            dma((chips,)),
            dma((chips,)),
            dma((chips,)),
            dma((3, half)),
            dma((4,)),
            dma((3, half)),
            dma((3, half)),
            dma((2, 2, half)),
            dma((2, 2, half)),
            dma((2, 2, 2, half)),
            dma((half,)),
            dma((half,)),
        ],
        compiler_params=pltpu.CompilerParams(
            collective_id=0, has_side_effects=True, vmem_limit_bytes=60 * 1024 * 1024
        ),
        cost_estimate=pl.CostEstimate(
            flops=4 * pairs * HD, bytes_accessed=60_000_000, transcendentals=pairs
        ),
    )(queries, key_rows, value_rows, tile_lists, tile_counts, out_weight)


def solution(mesh):
    in_specs = (
        P("dp", "ctx", None),
        P("dp", "ctx", None),
        P("dp", "ctx", None),
        P("dp", "ctx", None),
        P("dp", "ctx"),
        P("dp", None),
    )
    out_specs = P("dp", "ctx", None)
    return jax.shard_map(
        per_device, mesh=mesh, in_specs=in_specs, out_specs=out_specs, check_vma=False
    )
```

```python
import functools
import math

import jax
import jax.numpy as jnp
from jax import lax
from jax.experimental import pallas as pl
from jax.experimental.pallas import tpu as pltpu
from jax.sharding import PartitionSpec as P

HD = 128
REACH = 2
SLOTS = 5
WINDOW = 6
HIDDEN = -1e30
SHUT = 1e30
BLOCK = 256


def kernel(tiles, shards, q_ref, k_ref, v_ref, lists_ref, counts_ref, w_ref, out_ref,
           lists_held, counts_held, vis_mine, q_held, k_held, v_held, vis_held, done, stage, w_held, peak_kept, total_kept, mixture_kept, partial,
           w_own, w_send, w_recv, w_pass, w_core, own_sem, vis_sem, pair_send, pair_recv, own_send, pass_send, z_recv, back_send, back_recv):
    half = q_held.shape[1]
    me = lax.axis_index("ctx")
    row = lax.axis_index("dp")
    sibling = row + 1 - 2 * lax.rem(row, 2)
    depth = w_ref.shape[0]
    chips = shards // 2
    side = lax.rem(me, 2)
    pair = me + 1 - 2 * side
    has_up = me + 2 < tiles
    has_down = me >= 2
    up, down = me + 2, me - 2
    scale = math.log2(math.e) / math.sqrt(HD)

    def columns(ref, which, c):
        return ref.at[0, :, pl.ds(pl.multiple_of((which * half + c) * HD, HD), HD)]

    def remote(src, dst, send, recv, target):
        return pltpu.make_async_remote_copy(
            src_ref=src, dst_ref=dst, send_sem=send, recv_sem=recv,
            device_id={"ctx": target}, device_id_type=pl.DeviceIdType.MESH,
        )

    def to_pair(c):
        return [
            remote(columns(k_ref, 1 - side, c), k_held.at[2 + side, c], pair_send.at[0, c], pair_recv.at[0, c], pair),
            remote(columns(v_ref, 1 - side, c), v_held.at[2 + side, c], pair_send.at[1, c], pair_recv.at[1, c], pair),
            remote(columns(q_ref, 1 - side, c), q_held.at[side, c], pair_send.at[2, c], pair_recv.at[2, c], pair),
        ]

    def from_pair(c):
        other = 1 - side
        return [
            remote(columns(k_ref, side, c), k_held.at[2 + other, c], pair_send.at[0, c], pair_recv.at[0, c], pair),
            remote(columns(v_ref, side, c), v_held.at[2 + other, c], pair_send.at[1, c], pair_recv.at[1, c], pair),
            remote(columns(q_ref, side, c), q_held.at[other, c], pair_send.at[2, c], pair_recv.at[2, c], pair),
        ]

    def own_out(c, way):
        first, target = ((0, up), (4, down))[way]
        return [
            remote(columns(k_ref, side, c), k_held.at[first + side, c], own_send.at[way, 0, c], z_recv.at[way, 0, 0, c], target),
            remote(columns(v_ref, side, c), v_held.at[first + side, c], own_send.at[way, 1, c], z_recv.at[way, 0, 1, c], target),
        ]

    def pass_on(c, way):
        first, target = ((0, up), (4, down))[way]
        other = 1 - side
        return [
            remote(k_held.at[2 + other, c], k_held.at[first + other, c], pass_send.at[way, 0, c], z_recv.at[way, 1, 0, c], target),
            remote(v_held.at[2 + other, c], v_held.at[first + other, c], pass_send.at[way, 1, c], z_recv.at[way, 1, 1, c], target),
        ]

    def own_in(c):
        return [
            pltpu.make_async_copy(columns(q_ref, side, c), q_held.at[side, c], own_sem.at[0, c]),
            pltpu.make_async_copy(columns(k_ref, side, c), k_held.at[2 + side, c], own_sem.at[1, c]),
            pltpu.make_async_copy(columns(v_ref, side, c), v_held.at[2 + side, c], own_sem.at[2, c]),
        ]

    def head(which, c):
        return done.at[:, pl.ds(pl.multiple_of((which * half + c) * HD, HD), HD)]

    def back(c):
        return remote(stage.at[c], head(side, c), back_send.at[c], back_recv.at[c], pair)

    def shard(owner):
        return w_held.at[pl.ds(pl.multiple_of(owner * depth, depth), depth)]

    def w_copy(src, owner, send, recv, target):
        return pltpu.make_async_remote_copy(
            src_ref=src, dst_ref=shard(owner), send_sem=send, recv_sem=recv,
            device_id={"dp": target}, device_id_type=pl.DeviceIdType.MESH,
        )

    def w_chip(k):
        return w_copy(w_ref, row, w_send.at[k], w_recv.at[k], lax.rem(row + 2 * k, shards))

    def w_from(k):
        return lax.rem(row + shards - 2 * k, shards)

    def w_sibling(k):
        src = w_ref if k == 0 else shard(w_from(k))
        return w_copy(src, w_from(k), w_pass.at[k], w_core.at[k], sibling)

    w_in = pltpu.make_async_copy(w_ref, shard(row), w_own.at[0])

    lists_in = pltpu.make_async_copy(lists_ref, lists_held, vis_sem.at[0])
    counts_in = pltpu.make_async_copy(counts_ref, counts_held, vis_sem.at[3])
    vis_out = remote(vis_mine, vis_held.at[side], vis_sem.at[1], vis_sem.at[2], pair)
    vis_got = remote(vis_mine, vis_held.at[1 - side], vis_sem.at[1], vis_sem.at[2], pair)

    barrier = pltpu.get_barrier_semaphore()

    def greet(target):
        pl.semaphore_signal(barrier, inc=1, device_id={"ctx": target}, device_id_type=pl.DeviceIdType.MESH)

    def greet_row(target):
        pl.semaphore_signal(barrier, inc=1, device_id={"dp": target}, device_id_type=pl.DeviceIdType.MESH)

    greet(pair)
    greet_row(sibling)
    for k in range(1, chips):
        greet_row(lax.rem(row + 2 * k, shards))

    @pl.when(has_up)
    def _():
        greet(up)

    @pl.when(has_down)
    def _():
        greet(down)

    lists_in.start()
    counts_in.start()

    @pl.loop(0, half)
    def _(c):
        for copy in own_in(c):
            copy.start()

    pl.semaphore_wait(barrier, 1 + chips + has_up.astype(jnp.int32) + has_down.astype(jnp.int32))

    @pl.loop(0, half)
    def _(c):
        for copy in to_pair(c)[:2]:
            copy.start()

        @pl.when(has_up)
        def _():
            for copy in own_out(c, 0):
                copy.start()

        @pl.when(has_down)
        def _():
            for copy in own_out(c, 1):
                copy.start()

    w_in.start()
    for k in range(1, chips):
        w_chip(k).start()
    w_sibling(0).start()

    lists_in.wait()
    counts_in.wait()
    listed = lists_held[0]
    live = lax.broadcasted_iota(jnp.int32, listed.shape, 1) < counts_held[...]
    for o in range(SLOTS):
        match = jnp.where((listed == me + (o - REACH)) & live, 1.0, 0.0)
        row_seen = jnp.max(match, axis=1, keepdims=True)
        vis_mine[o : o + 1, :] = jnp.broadcast_to(row_seen, (1, HD))
        vis_held[side, o : o + 1, :] = jnp.broadcast_to(row_seen, (1, HD))
    vis_out.start()

    @pl.when(jnp.logical_not(has_down))
    def _():
        k_held[0:2] = jnp.zeros((2,) + k_held.shape[1:], k_held.dtype)
        v_held[0:2] = jnp.zeros((2,) + v_held.shape[1:], v_held.dtype)

    @pl.when(jnp.logical_not(has_up))
    def _():
        k_held[4:6] = jnp.zeros((2,) + k_held.shape[1:], k_held.dtype)
        v_held[4:6] = jnp.zeros((2,) + v_held.shape[1:], v_held.dtype)

    def attend(c, j, offsets, first):
        q = q_held[j, c]
        seen = [vis_held[j, pl.ds(o, 1), :] > 0.0 for o in offsets]
        scores, peak = [], None
        for o, see in zip(offsets, seen):
            s = lax.dot_general(q, k_held[j + o, c], (((1,), (1,)), ((), ())), preferred_element_type=jnp.float32)
            scores.append(s)
            top = s[:, :HD]
            for lane in range(HD, s.shape[1], HD):
                top = jnp.maximum(top, s[:, lane : lane + HD])
            top = jnp.where(see, top, HIDDEN)
            peak = top if peak is None else jnp.maximum(peak, top)
        peak = jnp.max(peak, axis=1, keepdims=True) * scale
        if first:
            total, mixture = None, None
        else:
            before = peak_kept[j, c][:, :1]
            peak = jnp.maximum(peak, before)
            fade = jnp.exp2(before - peak)
            total, mixture = total_kept[j, c] * fade, mixture_kept[j, c] * fade
        for o, see, s in zip(offsets, seen, scores):
            shift = jnp.where(see[:, :1], peak, SHUT)
            p = jnp.exp2(s * scale - shift)
            for lane in range(0, p.shape[1], HD):
                part = p[:, lane : lane + HD]
                total = part if total is None else total + part
            part = jnp.dot(p.astype(jnp.bfloat16), v_held[j + o, c], preferred_element_type=jnp.float32)
            mixture = part if mixture is None else mixture + part
        if first:
            peak_kept[j, c] = jnp.broadcast_to(peak, mixture.shape)
            total_kept[j, c] = total
            mixture_kept[j, c] = mixture
            return None
        total = jnp.sum(total, axis=1, keepdims=True)
        return (mixture / total).astype(jnp.bfloat16)

    early = (half - 2) * HD
    spans = [(0, early), (half * HD, half * HD + early)]
    rest = [(early, half * HD), (half * HD + early, 2 * half * HD)]

    def project(pieces, cols):
        return sum(
            jnp.dot(done[:, a:b], w_held[a:b, cols], preferred_element_type=jnp.float32) for a, b in pieces
        )

    @pl.loop(0, half)
    def _(c):
        for copy in from_pair(c)[:2]:
            copy.wait_recv()
        to_pair(c)[2].start()

        @pl.when(has_up)
        def _():
            for copy in pass_on(c, 0):
                copy.start()

        @pl.when(has_down)
        def _():
            for copy in pass_on(c, 1):
                copy.start()

        for copy in own_in(c):
            copy.wait()

        @pl.when(has_down)
        def _():
            for copy in own_out(c, 0):
                copy.wait_recv()

        @pl.when(has_up)
        def _():
            for copy in own_out(c, 1):
                copy.wait_recv()

        attend(c, side, [0, 2 - side, 3 - side, 4], True)

    vis_got.wait_recv()

    @pl.loop(0, half)
    def _(c):
        from_pair(c)[2].wait_recv()
        attend(c, 1 - side, [1, 2, 3], True)

        @pl.when(c == 1)
        def _():
            for k in range(1, chips):
                w_chip(k).wait_recv()
                w_sibling(k).start()

        @pl.when(c == half - 1)
        def _():
            w_in.wait()
            for k in range(chips):
                w_sibling(k).wait()
            for e in range(half - 2):
                back(e).wait_recv()

            @pl.loop(0, out_ref.shape[2] // BLOCK)
            def _(n):
                cols = pl.ds(pl.multiple_of(n * BLOCK, BLOCK), BLOCK)
                partial[:, cols] = project(spans, cols)

        @pl.when(has_down)
        def _():
            for copy in pass_on(c, 0):
                copy.wait_recv()

        @pl.when(has_up)
        def _():
            for copy in pass_on(c, 1):
                copy.wait_recv()

        stage[c] = attend(c, 1 - side, [0, 4], False)
        back(c).start()
        head(side, c)[...] = attend(c, side, [1 + 2 * side], False)

    for e in range(half - 2, half):
        back(e).wait_recv()

    @pl.loop(0, out_ref.shape[2] // BLOCK)
    def _(n):
        cols = pl.ds(pl.multiple_of(n * BLOCK, BLOCK), BLOCK)
        out_ref[0, :, cols] = (partial[:, cols] + project(rest, cols)).astype(jnp.bfloat16)

    @pl.loop(0, half)
    def _(c):
        for copy in to_pair(c):
            copy.wait_send()

        @pl.when(has_up)
        def _():
            for copy in own_out(c, 0) + pass_on(c, 0):
                copy.wait_send()

        @pl.when(has_down)
        def _():
            for copy in own_out(c, 1) + pass_on(c, 1):
                copy.wait_send()

        back(c).wait_send()

    for k in range(1, chips):
        w_chip(k).wait_send()
    vis_out.wait_send()


def per_device(queries, key_rows, value_rows, tile_lists, tile_counts, out_weight):
    tok_rows, channels = queries.shape[1], queries.shape[2]
    tiles = lax.axis_size("ctx")
    heads = channels // HD
    half = heads // 2
    hbm_spec = pl.BlockSpec(memory_space=pltpu.HBM)
    held = pltpu.VMEM((WINDOW, half, tok_rows, HD), jnp.bfloat16)
    kept = pltpu.VMEM((2, half, tok_rows, HD), jnp.float32)
    dma = pltpu.SemaphoreType.DMA
    pairs = 2 * tok_rows * SLOTS * tok_rows * half
    shards = lax.axis_size("dp")
    chips = shards // 2
    return pl.pallas_call(
        functools.partial(kernel, tiles, shards),
        out_shape=pltpu.VMEM((1, tok_rows, out_weight.shape[1]), jnp.bfloat16),
        in_specs=[hbm_spec] * 6,
        out_specs=pl.BlockSpec(memory_space=pltpu.VMEM),
        scratch_shapes=[
            pltpu.VMEM(tile_lists.shape, jnp.int32),
            pltpu.VMEM(tile_counts.shape, jnp.int32),
            pltpu.VMEM((8, HD), jnp.float32),
            pltpu.VMEM((2, half, tok_rows, HD), jnp.bfloat16),
            held,
            held,
            pltpu.VMEM((2, 8, HD), jnp.float32),
            pltpu.VMEM((tok_rows, channels), jnp.bfloat16),
            pltpu.VMEM((half, tok_rows, HD), jnp.bfloat16),
            pltpu.VMEM((channels, out_weight.shape[1]), jnp.bfloat16),
            kept,
            kept,
            kept,
            pltpu.VMEM((tok_rows, out_weight.shape[1]), jnp.float32),
            dma((1,)),
            dma((chips,)),
            dma((chips,)),
            dma((chips,)),
            dma((chips,)),
            dma((3, half)),
            dma((4,)),
            dma((3, half)),
            dma((3, half)),
            dma((2, 2, half)),
            dma((2, 2, half)),
            dma((2, 2, 2, half)),
            dma((half,)),
            dma((half,)),
        ],
        compiler_params=pltpu.CompilerParams(
            collective_id=0, has_side_effects=True, vmem_limit_bytes=60 * 1024 * 1024
        ),
        cost_estimate=pl.CostEstimate(
            flops=4 * pairs * HD, bytes_accessed=60_000_000, transcendentals=pairs
        ),
    )(queries, key_rows, value_rows, tile_lists, tile_counts, out_weight)


def solution(mesh):
    in_specs = (
        P("dp", "ctx", None),
        P("dp", "ctx", None),
        P("dp", "ctx", None),
        P("dp", "ctx", None),
        P("dp", "ctx"),
        P("dp", None),
    )
    out_specs = P("dp", "ctx", None)
    return jax.shard_map(
        per_device, mesh=mesh, in_specs=in_specs, out_specs=out_specs, check_vma=False
    )
```

```python
import functools
import math

import jax
import jax.numpy as jnp
from jax import lax
from jax.experimental import pallas as pl
from jax.experimental.pallas import tpu as pltpu
from jax.sharding import PartitionSpec as P

HD = 128
REACH = 2
SLOTS = 5
WINDOW = 6
HIDDEN = -1e30
SHUT = 1e30
BLOCK = 256
PIECES = 3


def kernel(tiles, shards, q_ref, k_ref, v_ref, lists_ref, counts_ref, w_ref, out_ref,
           lists_held, counts_held, vis_mine, q_held, k_held, v_held, vis_held, done, stage, w_held, peak_kept, total_kept, mixture_kept, partial,
           w_own, w_send, w_recv, w_pass, w_core, own_sem, vis_sem, pair_send, pair_recv, own_send, pass_send, z_recv, back_send, back_recv):
    half = q_held.shape[1]
    me = lax.axis_index("ctx")
    row = lax.axis_index("dp")
    sibling = row + 1 - 2 * lax.rem(row, 2)
    depth = w_ref.shape[0]
    chips = shards // 2
    side = lax.rem(me, 2)
    pair = me + 1 - 2 * side
    has_up = me + 2 < tiles
    has_down = me >= 2
    up, down = me + 2, me - 2
    scale = math.log2(math.e) / math.sqrt(HD)

    def columns(ref, which, c):
        return ref.at[0, :, pl.ds(pl.multiple_of((which * half + c) * HD, HD), HD)]

    def remote(src, dst, send, recv, target):
        return pltpu.make_async_remote_copy(
            src_ref=src, dst_ref=dst, send_sem=send, recv_sem=recv,
            device_id={"ctx": target}, device_id_type=pl.DeviceIdType.MESH,
        )

    def to_pair(c):
        return [
            remote(columns(k_ref, 1 - side, c), k_held.at[2 + side, c], pair_send.at[0, c], pair_recv.at[0, c], pair),
            remote(columns(v_ref, 1 - side, c), v_held.at[2 + side, c], pair_send.at[1, c], pair_recv.at[1, c], pair),
            remote(columns(q_ref, 1 - side, c), q_held.at[side, c], pair_send.at[2, c], pair_recv.at[2, c], pair),
        ]

    def from_pair(c):
        other = 1 - side
        return [
            remote(columns(k_ref, side, c), k_held.at[2 + other, c], pair_send.at[0, c], pair_recv.at[0, c], pair),
            remote(columns(v_ref, side, c), v_held.at[2 + other, c], pair_send.at[1, c], pair_recv.at[1, c], pair),
            remote(columns(q_ref, side, c), q_held.at[other, c], pair_send.at[2, c], pair_recv.at[2, c], pair),
        ]

    def own_out(c, way):
        first, target = ((0, up), (4, down))[way]
        return [
            remote(k_held.at[2 + side, c], k_held.at[first + side, c], own_send.at[way, 0, c], z_recv.at[way, 0, 0, c], target),
            remote(v_held.at[2 + side, c], v_held.at[first + side, c], own_send.at[way, 1, c], z_recv.at[way, 0, 1, c], target),
        ]

    def pass_on(c, way):
        first, target = ((0, up), (4, down))[way]
        other = 1 - side
        return [
            remote(k_held.at[2 + other, c], k_held.at[first + other, c], pass_send.at[way, 0, c], z_recv.at[way, 1, 0, c], target),
            remote(v_held.at[2 + other, c], v_held.at[first + other, c], pass_send.at[way, 1, c], z_recv.at[way, 1, 1, c], target),
        ]

    def own_in(c):
        return [
            pltpu.make_async_copy(columns(q_ref, side, c), q_held.at[side, c], own_sem.at[0, c]),
            pltpu.make_async_copy(columns(k_ref, side, c), k_held.at[2 + side, c], own_sem.at[1, c]),
            pltpu.make_async_copy(columns(v_ref, side, c), v_held.at[2 + side, c], own_sem.at[2, c]),
        ]

    def head(which, c):
        return done.at[:, pl.ds(pl.multiple_of((which * half + c) * HD, HD), HD)]

    def back(c):
        return remote(stage.at[c], head(side, c), back_send.at[c], back_recv.at[c], pair)

    slab = depth // PIECES

    def shard(owner, i):
        return w_held.at[pl.ds(pl.multiple_of(owner * depth + i * slab, slab), slab)]

    def mine(i):
        return w_ref.at[pl.ds(pl.multiple_of(i * slab, slab), slab)]

    def w_copy(src, owner, i, send, recv, target):
        return pltpu.make_async_remote_copy(
            src_ref=src, dst_ref=shard(owner, i), send_sem=send, recv_sem=recv,
            device_id={"dp": target}, device_id_type=pl.DeviceIdType.MESH,
        )

    def w_chip(k, i):
        return w_copy(mine(i), row, i, w_send.at[k, i], w_recv.at[k, i], lax.rem(row + 2 * k, shards))

    def w_from(k):
        return lax.rem(row + shards - 2 * k, shards)

    def w_sibling(k, i):
        src = mine(i) if k == 0 else shard(w_from(k), i)
        return w_copy(src, w_from(k), i, w_pass.at[k, i], w_core.at[k, i], sibling)

    w_in = pltpu.make_async_copy(w_ref, w_held.at[pl.ds(pl.multiple_of(row * depth, depth), depth)], w_own.at[0])

    lists_in = pltpu.make_async_copy(lists_ref, lists_held, vis_sem.at[0])
    counts_in = pltpu.make_async_copy(counts_ref, counts_held, vis_sem.at[3])
    vis_out = remote(vis_mine, vis_held.at[side], vis_sem.at[1], vis_sem.at[2], pair)
    vis_got = remote(vis_mine, vis_held.at[1 - side], vis_sem.at[1], vis_sem.at[2], pair)

    barrier = pltpu.get_barrier_semaphore()

    def greet(target):
        pl.semaphore_signal(barrier, inc=1, device_id={"ctx": target}, device_id_type=pl.DeviceIdType.MESH)

    def greet_row(target):
        pl.semaphore_signal(barrier, inc=1, device_id={"dp": target}, device_id_type=pl.DeviceIdType.MESH)

    greet(pair)
    greet_row(sibling)
    for k in range(1, chips):
        greet_row(lax.rem(row + 2 * k, shards))

    @pl.when(has_up)
    def _():
        greet(up)

    @pl.when(has_down)
    def _():
        greet(down)

    lists_in.start()
    counts_in.start()

    @pl.loop(0, half)
    def _(c):
        for copy in own_in(c):
            copy.start()

    pl.semaphore_wait(barrier, 1 + chips + has_up.astype(jnp.int32) + has_down.astype(jnp.int32))

    @pl.loop(0, half)
    def _(c):
        for copy in to_pair(c)[:2]:
            copy.start()
        for copy in own_in(c)[1:]:
            copy.wait()

        @pl.when(has_up)
        def _():
            for copy in own_out(c, 0):
                copy.start()

        @pl.when(has_down)
        def _():
            for copy in own_out(c, 1):
                copy.start()

    w_in.start()

    lists_in.wait()
    counts_in.wait()
    listed = lists_held[0]
    live = lax.broadcasted_iota(jnp.int32, listed.shape, 1) < counts_held[...]
    for o in range(SLOTS):
        match = jnp.where((listed == me + (o - REACH)) & live, 1.0, 0.0)
        row_seen = jnp.max(match, axis=1, keepdims=True)
        vis_mine[o : o + 1, :] = jnp.broadcast_to(row_seen, (1, HD))
        vis_held[side, o : o + 1, :] = jnp.broadcast_to(row_seen, (1, HD))
    vis_out.start()

    @pl.when(jnp.logical_not(has_down))
    def _():
        k_held[0:2] = jnp.zeros((2,) + k_held.shape[1:], k_held.dtype)
        v_held[0:2] = jnp.zeros((2,) + v_held.shape[1:], v_held.dtype)

    @pl.when(jnp.logical_not(has_up))
    def _():
        k_held[4:6] = jnp.zeros((2,) + k_held.shape[1:], k_held.dtype)
        v_held[4:6] = jnp.zeros((2,) + v_held.shape[1:], v_held.dtype)

    def attend(c, j, offsets, first):
        q = q_held[j, c]
        seen = [vis_held[j, pl.ds(o, 1), :] > 0.0 for o in offsets]
        scores, peak = [], None
        for o, see in zip(offsets, seen):
            s = lax.dot_general(q, k_held[j + o, c], (((1,), (1,)), ((), ())), preferred_element_type=jnp.float32)
            scores.append(s)
            top = s[:, :HD]
            for lane in range(HD, s.shape[1], HD):
                top = jnp.maximum(top, s[:, lane : lane + HD])
            top = jnp.where(see, top, HIDDEN)
            peak = top if peak is None else jnp.maximum(peak, top)
        peak = jnp.max(peak, axis=1, keepdims=True) * scale
        if first:
            total, mixture = None, None
        else:
            before = peak_kept[j, c][:, :1]
            peak = jnp.maximum(peak, before)
            fade = jnp.exp2(before - peak)
            total, mixture = total_kept[j, c] * fade, mixture_kept[j, c] * fade
        for o, see, s in zip(offsets, seen, scores):
            shift = jnp.where(see[:, :1], peak, SHUT)
            p = jnp.exp2(s * scale - shift)
            for lane in range(0, p.shape[1], HD):
                part = p[:, lane : lane + HD]
                total = part if total is None else total + part
            part = jnp.dot(p.astype(jnp.bfloat16), v_held[j + o, c], preferred_element_type=jnp.float32)
            mixture = part if mixture is None else mixture + part
        if first:
            peak_kept[j, c] = jnp.broadcast_to(peak, mixture.shape)
            total_kept[j, c] = total
            mixture_kept[j, c] = mixture
            return None
        total = jnp.sum(total, axis=1, keepdims=True)
        return (mixture / total).astype(jnp.bfloat16)

    early = (half - 2) * HD
    spans = [(0, early), (half * HD, half * HD + early)]
    rest = [(early, half * HD), (half * HD + early, 2 * half * HD)]

    def project(pieces, cols):
        return sum(
            jnp.dot(done[:, a:b], w_held[a:b, cols], preferred_element_type=jnp.float32) for a, b in pieces
        )

    @pl.loop(0, half)
    def _(c):
        for copy in from_pair(c)[:2]:
            copy.wait_recv()
        to_pair(c)[2].start()

        @pl.when(has_up)
        def _():
            for copy in pass_on(c, 0):
                copy.start()

        @pl.when(has_down)
        def _():
            for copy in pass_on(c, 1):
                copy.start()

        @pl.when(c < PIECES)
        def _():
            for k in range(1, chips):
                w_chip(k, c).start()
            w_sibling(0, c).start()

        own_in(c)[0].wait()

        @pl.when(has_down)
        def _():
            for copy in own_out(c, 0):
                copy.wait_recv()

        @pl.when(has_up)
        def _():
            for copy in own_out(c, 1):
                copy.wait_recv()

        attend(c, side, [0, 2 - side, 3 - side, 4], True)

    vis_got.wait_recv()

    @pl.loop(0, half)
    def _(c):
        from_pair(c)[2].wait_recv()
        attend(c, 1 - side, [1, 2, 3], True)

        @pl.when(c < PIECES)
        def _():
            for k in range(1, chips):
                w_chip(k, c).wait_recv()
                w_sibling(k, c).start()

        @pl.when(c == half - 1)
        def _():
            w_in.wait()
            for k in range(chips):
                for i in range(PIECES):
                    w_sibling(k, i).wait()
            for e in range(half - 2):
                back(e).wait_recv()

            @pl.loop(0, out_ref.shape[2] // BLOCK)
            def _(n):
                cols = pl.ds(pl.multiple_of(n * BLOCK, BLOCK), BLOCK)
                partial[:, cols] = project(spans, cols)

        @pl.when(has_down)
        def _():
            for copy in pass_on(c, 0):
                copy.wait_recv()

        @pl.when(has_up)
        def _():
            for copy in pass_on(c, 1):
                copy.wait_recv()

        stage[c] = attend(c, 1 - side, [0, 4], False)
        back(c).start()
        head(side, c)[...] = attend(c, side, [1 + 2 * side], False)

    for e in range(half - 2, half):
        back(e).wait_recv()

    @pl.loop(0, out_ref.shape[2] // BLOCK)
    def _(n):
        cols = pl.ds(pl.multiple_of(n * BLOCK, BLOCK), BLOCK)
        out_ref[0, :, cols] = (partial[:, cols] + project(rest, cols)).astype(jnp.bfloat16)

    @pl.loop(0, half)
    def _(c):
        for copy in to_pair(c):
            copy.wait_send()

        @pl.when(has_up)
        def _():
            for copy in own_out(c, 0) + pass_on(c, 0):
                copy.wait_send()

        @pl.when(has_down)
        def _():
            for copy in own_out(c, 1) + pass_on(c, 1):
                copy.wait_send()

        back(c).wait_send()

    for k in range(1, chips):
        for i in range(PIECES):
            w_chip(k, i).wait_send()
    vis_out.wait_send()


def per_device(queries, key_rows, value_rows, tile_lists, tile_counts, out_weight):
    tok_rows, channels = queries.shape[1], queries.shape[2]
    tiles = lax.axis_size("ctx")
    heads = channels // HD
    half = heads // 2
    hbm_spec = pl.BlockSpec(memory_space=pltpu.HBM)
    held = pltpu.VMEM((WINDOW, half, tok_rows, HD), jnp.bfloat16)
    kept = pltpu.VMEM((2, half, tok_rows, HD), jnp.float32)
    dma = pltpu.SemaphoreType.DMA
    pairs = 2 * tok_rows * SLOTS * tok_rows * half
    shards = lax.axis_size("dp")
    chips = shards // 2
    return pl.pallas_call(
        functools.partial(kernel, tiles, shards),
        out_shape=pltpu.VMEM((1, tok_rows, out_weight.shape[1]), jnp.bfloat16),
        in_specs=[hbm_spec] * 6,
        out_specs=pl.BlockSpec(memory_space=pltpu.VMEM),
        scratch_shapes=[
            pltpu.VMEM(tile_lists.shape, jnp.int32),
            pltpu.VMEM(tile_counts.shape, jnp.int32),
            pltpu.VMEM((8, HD), jnp.float32),
            pltpu.VMEM((2, half, tok_rows, HD), jnp.bfloat16),
            held,
            held,
            pltpu.VMEM((2, 8, HD), jnp.float32),
            pltpu.VMEM((tok_rows, channels), jnp.bfloat16),
            pltpu.VMEM((half, tok_rows, HD), jnp.bfloat16),
            pltpu.VMEM((channels, out_weight.shape[1]), jnp.bfloat16),
            kept,
            kept,
            kept,
            pltpu.VMEM((tok_rows, out_weight.shape[1]), jnp.float32),
            dma((1,)),
            dma((chips, PIECES)),
            dma((chips, PIECES)),
            dma((chips, PIECES)),
            dma((chips, PIECES)),
            dma((3, half)),
            dma((4,)),
            dma((3, half)),
            dma((3, half)),
            dma((2, 2, half)),
            dma((2, 2, half)),
            dma((2, 2, 2, half)),
            dma((half,)),
            dma((half,)),
        ],
        compiler_params=pltpu.CompilerParams(
            collective_id=0, has_side_effects=True, vmem_limit_bytes=60 * 1024 * 1024
        ),
        cost_estimate=pl.CostEstimate(
            flops=4 * pairs * HD, bytes_accessed=60_000_000, transcendentals=pairs
        ),
    )(queries, key_rows, value_rows, tile_lists, tile_counts, out_weight)


def solution(mesh):
    in_specs = (
        P("dp", "ctx", None),
        P("dp", "ctx", None),
        P("dp", "ctx", None),
        P("dp", "ctx", None),
        P("dp", "ctx"),
        P("dp", None),
    )
    out_specs = P("dp", "ctx", None)
    return jax.shard_map(
        per_device, mesh=mesh, in_specs=in_specs, out_specs=out_specs, check_vma=False
    )
```

```python
import functools
import math

import jax
import jax.numpy as jnp
from jax import lax
from jax.experimental import pallas as pl
from jax.experimental.pallas import tpu as pltpu
from jax.sharding import PartitionSpec as P

HD = 128
REACH = 2
SLOTS = 5
WINDOW = 6
HIDDEN = -1e30
SHUT = 1e30
BLOCK = 256
PIECES = 3
PARTS = 2


def kernel(tiles, shards, q_ref, k_ref, v_ref, lists_ref, counts_ref, w_ref, out_ref,
           lists_held, counts_held, vis_mine, q_held, k_held, v_held, vis_held, done, stage, w_held, peak_kept, total_kept, mixture_kept, partial,
           w_own, w_send, w_recv, w_pass, w_core, own_sem, vis_sem, pair_send, pair_recv, own_send, pass_send, z_recv, back_send, back_recv):
    half = q_held.shape[1]
    me = lax.axis_index("ctx")
    row = lax.axis_index("dp")
    sibling = row + 1 - 2 * lax.rem(row, 2)
    depth = w_ref.shape[0]
    chips = shards // 2
    side = lax.rem(me, 2)
    pair = me + 1 - 2 * side
    has_up = me + 2 < tiles
    has_down = me >= 2
    up, down = me + 2, me - 2
    scale = math.log2(math.e) / math.sqrt(HD)

    def columns(ref, which, c):
        return ref.at[0, :, pl.ds(pl.multiple_of((which * half + c) * HD, HD), HD)]

    def remote(src, dst, send, recv, target):
        return pltpu.make_async_remote_copy(
            src_ref=src, dst_ref=dst, send_sem=send, recv_sem=recv,
            device_id={"ctx": target}, device_id_type=pl.DeviceIdType.MESH,
        )

    def to_pair(c):
        return [
            remote(columns(k_ref, 1 - side, c), k_held.at[2 + side, c], pair_send.at[0, c], pair_recv.at[0, c], pair),
            remote(columns(v_ref, 1 - side, c), v_held.at[2 + side, c], pair_send.at[1, c], pair_recv.at[1, c], pair),
            remote(columns(q_ref, 1 - side, c), q_held.at[side, c], pair_send.at[2, c], pair_recv.at[2, c], pair),
        ]

    def from_pair(c):
        other = 1 - side
        return [
            remote(columns(k_ref, side, c), k_held.at[2 + other, c], pair_send.at[0, c], pair_recv.at[0, c], pair),
            remote(columns(v_ref, side, c), v_held.at[2 + other, c], pair_send.at[1, c], pair_recv.at[1, c], pair),
            remote(columns(q_ref, side, c), q_held.at[other, c], pair_send.at[2, c], pair_recv.at[2, c], pair),
        ]

    def own_out(c, way):
        first, target = ((0, up), (4, down))[way]
        return [
            remote(k_held.at[2 + side, c], k_held.at[first + side, c], own_send.at[way, 0, c], z_recv.at[way, 0, 0, c], target),
            remote(v_held.at[2 + side, c], v_held.at[first + side, c], own_send.at[way, 1, c], z_recv.at[way, 0, 1, c], target),
        ]

    def pass_on(c, way):
        first, target = ((0, up), (4, down))[way]
        other = 1 - side
        return [
            remote(k_held.at[2 + other, c], k_held.at[first + other, c], pass_send.at[way, 0, c], z_recv.at[way, 1, 0, c], target),
            remote(v_held.at[2 + other, c], v_held.at[first + other, c], pass_send.at[way, 1, c], z_recv.at[way, 1, 1, c], target),
        ]

    def own_in(c):
        return [
            pltpu.make_async_copy(columns(q_ref, side, c), q_held.at[side, c], own_sem.at[0, c]),
            pltpu.make_async_copy(columns(k_ref, side, c), k_held.at[2 + side, c], own_sem.at[1, c]),
            pltpu.make_async_copy(columns(v_ref, side, c), v_held.at[2 + side, c], own_sem.at[2, c]),
        ]

    def head(which, c):
        return done.at[:, pl.ds(pl.multiple_of((which * half + c) * HD, HD), HD)]

    part_rows = stage.shape[1] // PARTS

    def back(c, r):
        rows = slice(r * part_rows, (r + 1) * part_rows)
        return remote(
            stage.at[c, rows], done.at[rows, pl.ds(pl.multiple_of((side * half + c) * HD, HD), HD)],
            back_send.at[c, r], back_recv.at[c, r], pair,
        )

    slab = depth // PIECES

    def shard(owner, i):
        return w_held.at[pl.ds(pl.multiple_of(owner * depth + i * slab, slab), slab)]

    def mine(i):
        return w_ref.at[pl.ds(pl.multiple_of(i * slab, slab), slab)]

    def w_copy(src, owner, i, send, recv, target):
        return pltpu.make_async_remote_copy(
            src_ref=src, dst_ref=shard(owner, i), send_sem=send, recv_sem=recv,
            device_id={"dp": target}, device_id_type=pl.DeviceIdType.MESH,
        )

    def w_chip(k, i):
        return w_copy(mine(i), row, i, w_send.at[k, i], w_recv.at[k, i], lax.rem(row + 2 * k, shards))

    def w_from(k):
        return lax.rem(row + shards - 2 * k, shards)

    def w_sibling(k, i):
        src = mine(i) if k == 0 else shard(w_from(k), i)
        return w_copy(src, w_from(k), i, w_pass.at[k, i], w_core.at[k, i], sibling)

    w_in = pltpu.make_async_copy(w_ref, w_held.at[pl.ds(pl.multiple_of(row * depth, depth), depth)], w_own.at[0])

    lists_in = pltpu.make_async_copy(lists_ref, lists_held, vis_sem.at[0])
    counts_in = pltpu.make_async_copy(counts_ref, counts_held, vis_sem.at[3])
    vis_out = remote(vis_mine, vis_held.at[side], vis_sem.at[1], vis_sem.at[2], pair)
    vis_got = remote(vis_mine, vis_held.at[1 - side], vis_sem.at[1], vis_sem.at[2], pair)

    barrier = pltpu.get_barrier_semaphore()

    def greet(target):
        pl.semaphore_signal(barrier, inc=1, device_id={"ctx": target}, device_id_type=pl.DeviceIdType.MESH)

    def greet_row(target):
        pl.semaphore_signal(barrier, inc=1, device_id={"dp": target}, device_id_type=pl.DeviceIdType.MESH)

    greet(pair)
    greet_row(sibling)
    for k in range(1, chips):
        greet_row(lax.rem(row + 2 * k, shards))

    @pl.when(has_up)
    def _():
        greet(up)

    @pl.when(has_down)
    def _():
        greet(down)

    lists_in.start()
    counts_in.start()

    @pl.loop(0, half)
    def _(c):
        for copy in own_in(c):
            copy.start()

    pl.semaphore_wait(barrier, 1 + chips + has_up.astype(jnp.int32) + has_down.astype(jnp.int32))

    @pl.loop(0, half)
    def _(c):
        for copy in to_pair(c)[:2]:
            copy.start()
        for copy in own_in(c)[1:]:
            copy.wait()

        @pl.when(has_up)
        def _():
            for copy in own_out(c, 0):
                copy.start()

        @pl.when(has_down)
        def _():
            for copy in own_out(c, 1):
                copy.start()

    w_in.start()

    lists_in.wait()
    counts_in.wait()
    listed = lists_held[0]
    live = lax.broadcasted_iota(jnp.int32, listed.shape, 1) < counts_held[...]
    for o in range(SLOTS):
        match = jnp.where((listed == me + (o - REACH)) & live, 1.0, 0.0)
        row_seen = jnp.max(match, axis=1, keepdims=True)
        vis_mine[o : o + 1, :] = jnp.broadcast_to(row_seen, (1, HD))
        vis_held[side, o : o + 1, :] = jnp.broadcast_to(row_seen, (1, HD))
    vis_out.start()

    @pl.when(jnp.logical_not(has_down))
    def _():
        k_held[0:2] = jnp.zeros((2,) + k_held.shape[1:], k_held.dtype)
        v_held[0:2] = jnp.zeros((2,) + v_held.shape[1:], v_held.dtype)

    @pl.when(jnp.logical_not(has_up))
    def _():
        k_held[4:6] = jnp.zeros((2,) + k_held.shape[1:], k_held.dtype)
        v_held[4:6] = jnp.zeros((2,) + v_held.shape[1:], v_held.dtype)

    def attend(c, j, offsets, first, rows=slice(None), ready=None):
        q = q_held[j, c, rows]
        seen = [vis_held[j, pl.ds(o, 1), :] > 0.0 for o in offsets]
        scores, peak = [], None
        for o, see in zip(offsets, seen):
            s = lax.dot_general(q, k_held[j + o, c], (((1,), (1,)), ((), ())), preferred_element_type=jnp.float32)
            scores.append(s)
            top = s[:, :HD]
            for lane in range(HD, s.shape[1], HD):
                top = jnp.maximum(top, s[:, lane : lane + HD])
            top = jnp.where(see, top, HIDDEN)
            peak = top if peak is None else jnp.maximum(peak, top)
        peak = jnp.max(peak, axis=1, keepdims=True) * scale
        if first:
            total, mixture = None, None
        else:
            before = peak_kept[j, c, rows][:, :1]
            peak = jnp.maximum(peak, before)
            fade = jnp.exp2(before - peak)
            total, mixture = total_kept[j, c, rows] * fade, mixture_kept[j, c, rows] * fade
        if ready is not None:
            ready()
        for o, see, s in zip(offsets, seen, scores):
            shift = jnp.where(see[:, :1], peak, SHUT)
            p = jnp.exp2(s * scale - shift)
            for lane in range(0, p.shape[1], HD):
                part = p[:, lane : lane + HD]
                total = part if total is None else total + part
            part = jnp.dot(p.astype(jnp.bfloat16), v_held[j + o, c], preferred_element_type=jnp.float32)
            mixture = part if mixture is None else mixture + part
        if first:
            peak_kept[j, c] = jnp.broadcast_to(peak, mixture.shape)
            total_kept[j, c] = total
            mixture_kept[j, c] = mixture
            return None
        total = jnp.sum(total, axis=1, keepdims=True)
        return (mixture / total).astype(jnp.bfloat16)

    early = (half - 2) * HD
    spans = [(0, early), (half * HD, half * HD + early)]
    rest = [(early, half * HD), (half * HD + early, 2 * half * HD)]

    def project(pieces, cols, rows=slice(None)):
        return sum(
            jnp.dot(done[rows, a:b], w_held[a:b, cols], preferred_element_type=jnp.float32) for a, b in pieces
        )

    @pl.loop(0, half)
    def _(c):
        for copy in from_pair(c)[:2]:
            copy.wait_recv()
        to_pair(c)[2].start()

        @pl.when(has_up)
        def _():
            for copy in pass_on(c, 0):
                copy.start()

        @pl.when(has_down)
        def _():
            for copy in pass_on(c, 1):
                copy.start()

        @pl.when(c < PIECES)
        def _():
            for k in range(1, chips):
                w_chip(k, c).start()
            w_sibling(0, c).start()

        own_in(c)[0].wait()

        @pl.when(has_down)
        def _():
            for copy in own_out(c, 0):
                copy.wait_recv()

        @pl.when(has_up)
        def _():
            for copy in own_out(c, 1):
                copy.wait_recv()

        attend(c, side, [0, 2 - side, 3 - side, 4], True)

    vis_got.wait_recv()

    @pl.loop(0, half)
    def _(c):
        from_pair(c)[2].wait_recv()
        attend(c, 1 - side, [1, 2, 3], True)

        @pl.when(c < PIECES)
        def _():
            for k in range(1, chips):
                w_chip(k, c).wait_recv()
                w_sibling(k, c).start()

        @pl.when(c == half - 1)
        def _():
            w_in.wait()
            for k in range(chips):
                for i in range(PIECES):
                    w_sibling(k, i).wait()
            for e in range(half - 2):
                for r in range(PARTS):
                    back(e, r).wait_recv()

            @pl.loop(0, out_ref.shape[2] // BLOCK)
            def _(n):
                cols = pl.ds(pl.multiple_of(n * BLOCK, BLOCK), BLOCK)
                partial[:, cols] = project(spans, cols)

        def landed(which):
            @pl.when(has_down)
            def _():
                pass_on(c, 0)[which].wait_recv()

            @pl.when(has_up)
            def _():
                pass_on(c, 1)[which].wait_recv()

        landed(0)
        for r in range(PARTS):
            rows = slice(r * part_rows, (r + 1) * part_rows)
            stage[c, rows] = attend(
                c, 1 - side, [0, 4], False, rows, functools.partial(landed, 1) if r == 0 else None
            )
            back(c, r).start()
        head(side, c)[...] = attend(c, side, [1 + 2 * side], False)

    for r in range(PARTS):
        rows = slice(r * part_rows, (r + 1) * part_rows)
        for e in range(half - 2, half):
            back(e, r).wait_recv()

        @pl.loop(0, out_ref.shape[2] // BLOCK)
        def _(n):
            cols = pl.ds(pl.multiple_of(n * BLOCK, BLOCK), BLOCK)
            out_ref[0, rows, cols] = (partial[rows, cols] + project(rest, cols, rows)).astype(jnp.bfloat16)

    @pl.loop(0, half)
    def _(c):
        for copy in to_pair(c):
            copy.wait_send()

        @pl.when(has_up)
        def _():
            for copy in own_out(c, 0) + pass_on(c, 0):
                copy.wait_send()

        @pl.when(has_down)
        def _():
            for copy in own_out(c, 1) + pass_on(c, 1):
                copy.wait_send()

        for r in range(PARTS):
            back(c, r).wait_send()

    for k in range(1, chips):
        for i in range(PIECES):
            w_chip(k, i).wait_send()
    vis_out.wait_send()


def per_device(queries, key_rows, value_rows, tile_lists, tile_counts, out_weight):
    tok_rows, channels = queries.shape[1], queries.shape[2]
    tiles = lax.axis_size("ctx")
    heads = channels // HD
    half = heads // 2
    hbm_spec = pl.BlockSpec(memory_space=pltpu.HBM)
    held = pltpu.VMEM((WINDOW, half, tok_rows, HD), jnp.bfloat16)
    kept = pltpu.VMEM((2, half, tok_rows, HD), jnp.float32)
    dma = pltpu.SemaphoreType.DMA
    pairs = 2 * tok_rows * SLOTS * tok_rows * half
    shards = lax.axis_size("dp")
    chips = shards // 2
    return pl.pallas_call(
        functools.partial(kernel, tiles, shards),
        out_shape=pltpu.VMEM((1, tok_rows, out_weight.shape[1]), jnp.bfloat16),
        in_specs=[hbm_spec] * 6,
        out_specs=pl.BlockSpec(memory_space=pltpu.VMEM),
        scratch_shapes=[
            pltpu.VMEM(tile_lists.shape, jnp.int32),
            pltpu.VMEM(tile_counts.shape, jnp.int32),
            pltpu.VMEM((8, HD), jnp.float32),
            pltpu.VMEM((2, half, tok_rows, HD), jnp.bfloat16),
            held,
            held,
            pltpu.VMEM((2, 8, HD), jnp.float32),
            pltpu.VMEM((tok_rows, channels), jnp.bfloat16),
            pltpu.VMEM((half, tok_rows, HD), jnp.bfloat16),
            pltpu.VMEM((channels, out_weight.shape[1]), jnp.bfloat16),
            kept,
            kept,
            kept,
            pltpu.VMEM((tok_rows, out_weight.shape[1]), jnp.float32),
            dma((1,)),
            dma((chips, PIECES)),
            dma((chips, PIECES)),
            dma((chips, PIECES)),
            dma((chips, PIECES)),
            dma((3, half)),
            dma((4,)),
            dma((3, half)),
            dma((3, half)),
            dma((2, 2, half)),
            dma((2, 2, half)),
            dma((2, 2, 2, half)),
            dma((half, PARTS)),
            dma((half, PARTS)),
        ],
        compiler_params=pltpu.CompilerParams(
            collective_id=0, has_side_effects=True, vmem_limit_bytes=60 * 1024 * 1024
        ),
        cost_estimate=pl.CostEstimate(
            flops=4 * pairs * HD, bytes_accessed=60_000_000, transcendentals=pairs
        ),
    )(queries, key_rows, value_rows, tile_lists, tile_counts, out_weight)


def solution(mesh):
    in_specs = (
        P("dp", "ctx", None),
        P("dp", "ctx", None),
        P("dp", "ctx", None),
        P("dp", "ctx", None),
        P("dp", "ctx"),
        P("dp", None),
    )
    out_specs = P("dp", "ctx", None)
    return jax.shard_map(
        per_device, mesh=mesh, in_specs=in_specs, out_specs=out_specs, check_vma=False
    )
```

```python
import functools
import math

import jax
import jax.numpy as jnp
from jax import lax
from jax.experimental import pallas as pl
from jax.experimental.pallas import tpu as pltpu
from jax.sharding import PartitionSpec as P

HD = 128
REACH = 2
SLOTS = 5
WINDOW = 6
HIDDEN = -1e30
SHUT = 1e30
BLOCK = 256
PIECES = 3
AHEAD = 2


def kernel(tiles, shards, q_ref, k_ref, v_ref, lists_ref, counts_ref, w_ref, out_ref,
           lists_held, counts_held, vis_mine, q_held, k_held, v_held, vis_held, done, stage, w_held, peak_kept, total_kept, mixture_kept, partial,
           w_own, w_send, w_recv, w_pass, w_core, own_sem, vis_sem, pair_send, pair_recv, own_send, pass_send, z_recv, back_send, back_recv):
    half = q_held.shape[1]
    me = lax.axis_index("ctx")
    row = lax.axis_index("dp")
    sibling = row + 1 - 2 * lax.rem(row, 2)
    depth = w_ref.shape[0]
    chips = shards // 2
    side = lax.rem(me, 2)
    pair = me + 1 - 2 * side
    has_up = me + 2 < tiles
    has_down = me >= 2
    up, down = me + 2, me - 2
    scale = math.log2(math.e) / math.sqrt(HD)

    def columns(ref, which, c):
        return ref.at[0, :, pl.ds(pl.multiple_of((which * half + c) * HD, HD), HD)]

    def remote(src, dst, send, recv, target):
        return pltpu.make_async_remote_copy(
            src_ref=src, dst_ref=dst, send_sem=send, recv_sem=recv,
            device_id={"ctx": target}, device_id_type=pl.DeviceIdType.MESH,
        )

    def to_pair(c):
        return [
            remote(columns(k_ref, 1 - side, c), k_held.at[2 + side, c], pair_send.at[0, c], pair_recv.at[0, c], pair),
            remote(columns(v_ref, 1 - side, c), v_held.at[2 + side, c], pair_send.at[1, c], pair_recv.at[1, c], pair),
            remote(columns(q_ref, 1 - side, c), q_held.at[side, c], pair_send.at[2, c], pair_recv.at[2, c], pair),
        ]

    def from_pair(c):
        other = 1 - side
        return [
            remote(columns(k_ref, side, c), k_held.at[2 + other, c], pair_send.at[0, c], pair_recv.at[0, c], pair),
            remote(columns(v_ref, side, c), v_held.at[2 + other, c], pair_send.at[1, c], pair_recv.at[1, c], pair),
            remote(columns(q_ref, side, c), q_held.at[other, c], pair_send.at[2, c], pair_recv.at[2, c], pair),
        ]

    def own_out(c, way):
        first, target = ((0, up), (4, down))[way]
        return [
            remote(k_held.at[2 + side, c], k_held.at[first + side, c], own_send.at[way, 0, c], z_recv.at[way, 0, 0, c], target),
            remote(v_held.at[2 + side, c], v_held.at[first + side, c], own_send.at[way, 1, c], z_recv.at[way, 0, 1, c], target),
        ]

    def pass_on(c, way):
        first, target = ((0, up), (4, down))[way]
        other = 1 - side
        return [
            remote(k_held.at[2 + other, c], k_held.at[first + other, c], pass_send.at[way, 0, c], z_recv.at[way, 1, 0, c], target),
            remote(v_held.at[2 + other, c], v_held.at[first + other, c], pass_send.at[way, 1, c], z_recv.at[way, 1, 1, c], target),
        ]

    def own_in(c):
        return [
            pltpu.make_async_copy(columns(q_ref, side, c), q_held.at[side, c], own_sem.at[0, c]),
            pltpu.make_async_copy(columns(k_ref, side, c), k_held.at[2 + side, c], own_sem.at[1, c]),
            pltpu.make_async_copy(columns(v_ref, side, c), v_held.at[2 + side, c], own_sem.at[2, c]),
        ]

    def head(which, c):
        return done.at[:, pl.ds(pl.multiple_of((which * half + c) * HD, HD), HD)]

    def back(c):
        return remote(stage.at[c], head(side, c), back_send.at[c], back_recv.at[c], pair)

    slab = depth // PIECES

    def shard(owner, i):
        return w_held.at[pl.ds(pl.multiple_of(owner * depth + i * slab, slab), slab)]

    def mine(i):
        return w_ref.at[pl.ds(pl.multiple_of(i * slab, slab), slab)]

    def w_copy(src, owner, i, send, recv, target):
        return pltpu.make_async_remote_copy(
            src_ref=src, dst_ref=shard(owner, i), send_sem=send, recv_sem=recv,
            device_id={"dp": target}, device_id_type=pl.DeviceIdType.MESH,
        )

    def w_chip(k, i):
        return w_copy(mine(i), row, i, w_send.at[k, i], w_recv.at[k, i], lax.rem(row + 2 * k, shards))

    def w_from(k):
        return lax.rem(row + shards - 2 * k, shards)

    def w_sibling(k, i):
        src = mine(i) if k == 0 else shard(w_from(k), i)
        return w_copy(src, w_from(k), i, w_pass.at[k, i], w_core.at[k, i], sibling)

    w_in = pltpu.make_async_copy(w_ref, w_held.at[pl.ds(pl.multiple_of(row * depth, depth), depth)], w_own.at[0])

    lists_in = pltpu.make_async_copy(lists_ref, lists_held, vis_sem.at[0])
    counts_in = pltpu.make_async_copy(counts_ref, counts_held, vis_sem.at[3])
    vis_out = remote(vis_mine, vis_held.at[side], vis_sem.at[1], vis_sem.at[2], pair)
    vis_got = remote(vis_mine, vis_held.at[1 - side], vis_sem.at[1], vis_sem.at[2], pair)

    barrier = pltpu.get_barrier_semaphore()

    def greet(target):
        pl.semaphore_signal(barrier, inc=1, device_id={"ctx": target}, device_id_type=pl.DeviceIdType.MESH)

    def greet_row(target):
        pl.semaphore_signal(barrier, inc=1, device_id={"dp": target}, device_id_type=pl.DeviceIdType.MESH)

    greet(pair)
    greet_row(sibling)
    for k in range(1, chips):
        greet_row(lax.rem(row + 2 * k, shards))

    @pl.when(has_up)
    def _():
        greet(up)

    @pl.when(has_down)
    def _():
        greet(down)

    lists_in.start()
    counts_in.start()

    @pl.loop(0, half)
    def _(c):
        for copy in own_in(c):
            copy.start()

    pl.semaphore_wait(barrier, 1 + chips + has_up.astype(jnp.int32) + has_down.astype(jnp.int32))

    @pl.loop(0, half)
    def _(c):
        for copy in to_pair(c)[:2]:
            copy.start()
        for copy in own_in(c)[1:]:
            copy.wait()

        @pl.when(has_up)
        def _():
            for copy in own_out(c, 0):
                copy.start()

        @pl.when(has_down)
        def _():
            for copy in own_out(c, 1):
                copy.start()

    w_in.start()

    lists_in.wait()
    counts_in.wait()
    listed = lists_held[0]
    live = lax.broadcasted_iota(jnp.int32, listed.shape, 1) < counts_held[...]
    for o in range(SLOTS):
        match = jnp.where((listed == me + (o - REACH)) & live, 1.0, 0.0)
        row_seen = jnp.max(match, axis=1, keepdims=True)
        vis_mine[o : o + 1, :] = jnp.broadcast_to(row_seen, (1, HD))
        vis_held[side, o : o + 1, :] = jnp.broadcast_to(row_seen, (1, HD))
    vis_out.start()

    @pl.when(jnp.logical_not(has_down))
    def _():
        k_held[0:2] = jnp.zeros((2,) + k_held.shape[1:], k_held.dtype)
        v_held[0:2] = jnp.zeros((2,) + v_held.shape[1:], v_held.dtype)

    @pl.when(jnp.logical_not(has_up))
    def _():
        k_held[4:6] = jnp.zeros((2,) + k_held.shape[1:], k_held.dtype)
        v_held[4:6] = jnp.zeros((2,) + v_held.shape[1:], v_held.dtype)

    def attend(c, j, offsets, first):
        q = q_held[j, c]
        seen = [vis_held[j, pl.ds(o, 1), :] > 0.0 for o in offsets]
        scores, peak = [], None
        for o, see in zip(offsets, seen):
            s = lax.dot_general(q, k_held[j + o, c], (((1,), (1,)), ((), ())), preferred_element_type=jnp.float32)
            scores.append(s)
            top = s[:, :HD]
            for lane in range(HD, s.shape[1], HD):
                top = jnp.maximum(top, s[:, lane : lane + HD])
            top = jnp.where(see, top, HIDDEN)
            peak = top if peak is None else jnp.maximum(peak, top)
        peak = jnp.max(peak, axis=1, keepdims=True) * scale
        if first:
            total, mixture = None, None
        else:
            before = peak_kept[j, c][:, :1]
            peak = jnp.maximum(peak, before)
            fade = jnp.exp2(before - peak)
            total, mixture = total_kept[j, c] * fade, mixture_kept[j, c] * fade
        for o, see, s in zip(offsets, seen, scores):
            shift = jnp.where(see[:, :1], peak, SHUT)
            p = jnp.exp2(s * scale - shift)
            for lane in range(0, p.shape[1], HD):
                part = p[:, lane : lane + HD]
                total = part if total is None else total + part
            part = jnp.dot(p.astype(jnp.bfloat16), v_held[j + o, c], preferred_element_type=jnp.float32)
            mixture = part if mixture is None else mixture + part
        if first:
            peak_kept[j, c] = jnp.broadcast_to(peak, mixture.shape)
            total_kept[j, c] = total
            mixture_kept[j, c] = mixture
            return None
        total = jnp.sum(total, axis=1, keepdims=True)
        return (mixture / total).astype(jnp.bfloat16)

    third = half // 3

    def project(part, cols):
        total = None
        for a in (part * third * HD, (half + part * third) * HD):
            b = a + third * HD
            product = jnp.dot(done[:, a:b], w_held[a:b, cols], preferred_element_type=jnp.float32)
            total = product if total is None else total + product
        return total

    def returned(part):
        for e in range(part * third, (part + 1) * third):
            back(e).wait_recv()

    def forward(c):
        for copy in from_pair(c)[:2]:
            copy.wait_recv()
        to_pair(c)[2].start()

        @pl.when(has_up)
        def _():
            for copy in pass_on(c, 0):
                copy.start()

        @pl.when(has_down)
        def _():
            for copy in pass_on(c, 1):
                copy.start()

    for c in range(AHEAD):
        forward(c)

    @pl.loop(0, half)
    def _(c):
        @pl.when(c + AHEAD < half)
        def _():
            forward(c + AHEAD)

        @pl.when(c < PIECES)
        def _():
            for k in range(1, chips):
                w_chip(k, c).start()
            w_sibling(0, c).start()

        own_in(c)[0].wait()

        @pl.when(has_down)
        def _():
            for copy in own_out(c, 0):
                copy.wait_recv()

        @pl.when(has_up)
        def _():
            for copy in own_out(c, 1):
                copy.wait_recv()

        attend(c, side, [0, 2 - side, 3 - side, 4], True)

    vis_got.wait_recv()

    @pl.loop(0, half)
    def _(c):
        from_pair(c)[2].wait_recv()
        attend(c, 1 - side, [1, 2, 3], True)

    @pl.loop(0, half)
    def _(c):
        @pl.when(c < PIECES)
        def _():
            for k in range(1, chips):
                w_chip(k, c).wait_recv()
                w_sibling(k, c).start()

        @pl.when(c == half - third)
        def _():
            w_in.wait()
            for k in range(chips):
                for i in range(PIECES):
                    w_sibling(k, i).wait()
            returned(0)

            @pl.loop(0, out_ref.shape[2] // BLOCK)
            def _(n):
                cols = pl.ds(pl.multiple_of(n * BLOCK, BLOCK), BLOCK)
                partial[:, cols] = project(0, cols)

        @pl.when(has_down)
        def _():
            for copy in pass_on(c, 0):
                copy.wait_recv()

        @pl.when(has_up)
        def _():
            for copy in pass_on(c, 1):
                copy.wait_recv()

        stage[c] = attend(c, 1 - side, [0, 4], False)
        back(c).start()
        head(side, c)[...] = attend(c, side, [1 + 2 * side], False)

    returned(1)

    @pl.loop(0, out_ref.shape[2] // BLOCK)
    def _(n):
        cols = pl.ds(pl.multiple_of(n * BLOCK, BLOCK), BLOCK)
        partial[:, cols] += project(1, cols)

    returned(2)

    @pl.loop(0, out_ref.shape[2] // BLOCK)
    def _(n):
        cols = pl.ds(pl.multiple_of(n * BLOCK, BLOCK), BLOCK)
        out_ref[0, :, cols] = (partial[:, cols] + project(2, cols)).astype(jnp.bfloat16)

    @pl.loop(0, half)
    def _(c):
        for copy in to_pair(c):
            copy.wait_send()

        @pl.when(has_up)
        def _():
            for copy in own_out(c, 0) + pass_on(c, 0):
                copy.wait_send()

        @pl.when(has_down)
        def _():
            for copy in own_out(c, 1) + pass_on(c, 1):
                copy.wait_send()

        back(c).wait_send()

    for k in range(1, chips):
        for i in range(PIECES):
            w_chip(k, i).wait_send()
    vis_out.wait_send()


def per_device(queries, key_rows, value_rows, tile_lists, tile_counts, out_weight):
    tok_rows, channels = queries.shape[1], queries.shape[2]
    tiles = lax.axis_size("ctx")
    heads = channels // HD
    half = heads // 2
    hbm_spec = pl.BlockSpec(memory_space=pltpu.HBM)
    held = pltpu.VMEM((WINDOW, half, tok_rows, HD), jnp.bfloat16)
    kept = pltpu.VMEM((2, half, tok_rows, HD), jnp.float32)
    dma = pltpu.SemaphoreType.DMA
    pairs = 2 * tok_rows * SLOTS * tok_rows * half
    shards = lax.axis_size("dp")
    chips = shards // 2
    return pl.pallas_call(
        functools.partial(kernel, tiles, shards),
        out_shape=pltpu.VMEM((1, tok_rows, out_weight.shape[1]), jnp.bfloat16),
        in_specs=[hbm_spec] * 6,
        out_specs=pl.BlockSpec(memory_space=pltpu.VMEM),
        scratch_shapes=[
            pltpu.VMEM(tile_lists.shape, jnp.int32),
            pltpu.VMEM(tile_counts.shape, jnp.int32),
            pltpu.VMEM((8, HD), jnp.float32),
            pltpu.VMEM((2, half, tok_rows, HD), jnp.bfloat16),
            held,
            held,
            pltpu.VMEM((2, 8, HD), jnp.float32),
            pltpu.VMEM((tok_rows, channels), jnp.bfloat16),
            pltpu.VMEM((half, tok_rows, HD), jnp.bfloat16),
            pltpu.VMEM((channels, out_weight.shape[1]), jnp.bfloat16),
            kept,
            kept,
            kept,
            pltpu.VMEM((tok_rows, out_weight.shape[1]), jnp.float32),
            dma((1,)),
            dma((chips, PIECES)),
            dma((chips, PIECES)),
            dma((chips, PIECES)),
            dma((chips, PIECES)),
            dma((3, half)),
            dma((4,)),
            dma((3, half)),
            dma((3, half)),
            dma((2, 2, half)),
            dma((2, 2, half)),
            dma((2, 2, 2, half)),
            dma((half,)),
            dma((half,)),
        ],
        compiler_params=pltpu.CompilerParams(
            collective_id=0, has_side_effects=True, vmem_limit_bytes=60 * 1024 * 1024
        ),
        cost_estimate=pl.CostEstimate(
            flops=4 * pairs * HD, bytes_accessed=60_000_000, transcendentals=pairs
        ),
    )(queries, key_rows, value_rows, tile_lists, tile_counts, out_weight)


def solution(mesh):
    in_specs = (
        P("dp", "ctx", None),
        P("dp", "ctx", None),
        P("dp", "ctx", None),
        P("dp", "ctx", None),
        P("dp", "ctx"),
        P("dp", None),
    )
    out_specs = P("dp", "ctx", None)
    return jax.shard_map(
        per_device, mesh=mesh, in_specs=in_specs, out_specs=out_specs, check_vma=False
    )
```

```python
import functools
import math

import jax
import jax.numpy as jnp
from jax import lax
from jax.experimental import pallas as pl
from jax.experimental.pallas import tpu as pltpu
from jax.sharding import PartitionSpec as P

HD = 128
REACH = 2
SLOTS = 5
WINDOW = 6
HIDDEN = -1e30
SHUT = 1e30
BLOCK = 256
PIECES = 3
AHEAD = 2


def kernel(tiles, shards, q_ref, k_ref, v_ref, lists_ref, counts_ref, w_ref, out_ref,
           lists_held, counts_held, vis_mine, q_held, k_held, v_held, vis_held, done, stage, w_held, peak_kept, total_kept, mixture_kept, partial,
           w_own, w_send, w_recv, w_pass, w_core, own_sem, vis_sem, pair_send, pair_recv, own_send, pass_send, z_recv, back_send, back_recv):
    half = q_held.shape[1]
    me = lax.axis_index("ctx")
    row = lax.axis_index("dp")
    sibling = row + 1 - 2 * lax.rem(row, 2)
    depth = w_ref.shape[0]
    chips = shards // 2
    side = lax.rem(me, 2)
    pair = me + 1 - 2 * side
    has_up = me + 2 < tiles
    has_down = me >= 2
    up, down = me + 2, me - 2
    scale = math.log2(math.e) / math.sqrt(HD)

    def columns(ref, which, c):
        return ref.at[0, :, pl.ds(pl.multiple_of((which * half + c) * HD, HD), HD)]

    def remote(src, dst, send, recv, target):
        return pltpu.make_async_remote_copy(
            src_ref=src, dst_ref=dst, send_sem=send, recv_sem=recv,
            device_id={"ctx": target}, device_id_type=pl.DeviceIdType.MESH,
        )

    def to_pair(c):
        return [
            remote(columns(k_ref, 1 - side, c), k_held.at[2 + side, c], pair_send.at[0, c], pair_recv.at[0, c], pair),
            remote(columns(v_ref, 1 - side, c), v_held.at[2 + side, c], pair_send.at[1, c], pair_recv.at[1, c], pair),
            remote(columns(q_ref, 1 - side, c), q_held.at[side, c], pair_send.at[2, c], pair_recv.at[2, c], pair),
        ]

    def from_pair(c):
        other = 1 - side
        return [
            remote(columns(k_ref, side, c), k_held.at[2 + other, c], pair_send.at[0, c], pair_recv.at[0, c], pair),
            remote(columns(v_ref, side, c), v_held.at[2 + other, c], pair_send.at[1, c], pair_recv.at[1, c], pair),
            remote(columns(q_ref, side, c), q_held.at[other, c], pair_send.at[2, c], pair_recv.at[2, c], pair),
        ]

    def own_out(c, way):
        first, target = ((0, up), (4, down))[way]
        return [
            remote(k_held.at[2 + side, c], k_held.at[first + side, c], own_send.at[way, 0, c], z_recv.at[way, 0, 0, c], target),
            remote(v_held.at[2 + side, c], v_held.at[first + side, c], own_send.at[way, 1, c], z_recv.at[way, 0, 1, c], target),
        ]

    def pass_on(c, way):
        first, target = ((0, up), (4, down))[way]
        other = 1 - side
        return [
            remote(k_held.at[2 + other, c], k_held.at[first + other, c], pass_send.at[way, 0, c], z_recv.at[way, 1, 0, c], target),
            remote(v_held.at[2 + other, c], v_held.at[first + other, c], pass_send.at[way, 1, c], z_recv.at[way, 1, 1, c], target),
        ]

    def own_in(c):
        return [
            pltpu.make_async_copy(columns(q_ref, side, c), q_held.at[side, c], own_sem.at[0, c]),
            pltpu.make_async_copy(columns(k_ref, side, c), k_held.at[2 + side, c], own_sem.at[1, c]),
            pltpu.make_async_copy(columns(v_ref, side, c), v_held.at[2 + side, c], own_sem.at[2, c]),
        ]

    def head(which, c):
        return done.at[:, pl.ds(pl.multiple_of((which * half + c) * HD, HD), HD)]

    def back(c):
        return remote(stage.at[c], head(side, c), back_send.at[c], back_recv.at[c], pair)

    slab = depth // PIECES

    def shard(owner, i):
        return w_held.at[pl.ds(pl.multiple_of(owner * depth + i * slab, slab), slab)]

    def mine(i):
        return w_ref.at[pl.ds(pl.multiple_of(i * slab, slab), slab)]

    def w_copy(src, owner, i, send, recv, target):
        return pltpu.make_async_remote_copy(
            src_ref=src, dst_ref=shard(owner, i), send_sem=send, recv_sem=recv,
            device_id={"dp": target}, device_id_type=pl.DeviceIdType.MESH,
        )

    def w_chip(k, i):
        return w_copy(mine(i), row, i, w_send.at[k, i], w_recv.at[k, i], lax.rem(row + 2 * k, shards))

    def w_from(k):
        return lax.rem(row + shards - 2 * k, shards)

    def w_sibling(k, i):
        src = mine(i) if k == 0 else shard(w_from(k), i)
        return w_copy(src, w_from(k), i, w_pass.at[k, i], w_core.at[k, i], sibling)

    w_in = pltpu.make_async_copy(w_ref, w_held.at[pl.ds(pl.multiple_of(row * depth, depth), depth)], w_own.at[0])

    lists_in = pltpu.make_async_copy(lists_ref, lists_held, vis_sem.at[0])
    counts_in = pltpu.make_async_copy(counts_ref, counts_held, vis_sem.at[3])
    vis_out = remote(vis_mine, vis_held.at[side], vis_sem.at[1], vis_sem.at[2], pair)
    vis_got = remote(vis_mine, vis_held.at[1 - side], vis_sem.at[1], vis_sem.at[2], pair)

    barrier = pltpu.get_barrier_semaphore()

    def greet(target):
        pl.semaphore_signal(barrier, inc=1, device_id={"ctx": target}, device_id_type=pl.DeviceIdType.MESH)

    def greet_row(target):
        pl.semaphore_signal(barrier, inc=1, device_id={"dp": target}, device_id_type=pl.DeviceIdType.MESH)

    greet(pair)
    greet_row(sibling)
    for k in range(1, chips):
        greet_row(lax.rem(row + 2 * k, shards))

    @pl.when(has_up)
    def _():
        greet(up)

    @pl.when(has_down)
    def _():
        greet(down)

    lists_in.start()
    counts_in.start()

    @pl.loop(0, half)
    def _(c):
        for copy in own_in(c):
            copy.start()

    pl.semaphore_wait(barrier, 1 + chips + has_up.astype(jnp.int32) + has_down.astype(jnp.int32))

    @pl.loop(0, half)
    def _(c):
        for copy in to_pair(c)[:2]:
            copy.start()
        for copy in own_in(c)[1:]:
            copy.wait()

        @pl.when(has_up)
        def _():
            for copy in own_out(c, 0):
                copy.start()

        @pl.when(has_down)
        def _():
            for copy in own_out(c, 1):
                copy.start()

    w_in.start()

    lists_in.wait()
    counts_in.wait()
    listed = lists_held[0]
    live = lax.broadcasted_iota(jnp.int32, listed.shape, 1) < counts_held[...]
    for o in range(SLOTS):
        match = jnp.where((listed == me + (o - REACH)) & live, 1.0, 0.0)
        row_seen = jnp.max(match, axis=1, keepdims=True)
        vis_mine[o : o + 1, :] = jnp.broadcast_to(row_seen, (1, HD))
        vis_held[side, o : o + 1, :] = jnp.broadcast_to(row_seen, (1, HD))
    vis_out.start()

    @pl.when(jnp.logical_not(has_down))
    def _():
        k_held[0:2] = jnp.zeros((2,) + k_held.shape[1:], k_held.dtype)
        v_held[0:2] = jnp.zeros((2,) + v_held.shape[1:], v_held.dtype)

    @pl.when(jnp.logical_not(has_up))
    def _():
        k_held[4:6] = jnp.zeros((2,) + k_held.shape[1:], k_held.dtype)
        v_held[4:6] = jnp.zeros((2,) + v_held.shape[1:], v_held.dtype)

    def attend(c, j, offsets, first):
        q = q_held[j, c]
        seen = [vis_held[j, pl.ds(o, 1), :] > 0.0 for o in offsets]
        scores, peak = [], None
        for o, see in zip(offsets, seen):
            s = lax.dot_general(q, k_held[j + o, c], (((1,), (1,)), ((), ())), preferred_element_type=jnp.float32)
            scores.append(s)
            top = s[:, :HD]
            for lane in range(HD, s.shape[1], HD):
                top = jnp.maximum(top, s[:, lane : lane + HD])
            top = jnp.where(see, top, HIDDEN)
            peak = top if peak is None else jnp.maximum(peak, top)
        peak = jnp.max(peak, axis=1, keepdims=True) * scale
        if first:
            total, mixture = None, None
        else:
            before = peak_kept[j, c][:, :1]
            peak = jnp.maximum(peak, before)
            fade = jnp.exp2(before - peak)
            total, mixture = total_kept[j, c] * fade, mixture_kept[j, c] * fade
        for o, see, s in zip(offsets, seen, scores):
            shift = jnp.where(see[:, :1], peak, SHUT)
            p = jnp.exp2(s * scale - shift)
            for lane in range(0, p.shape[1], HD):
                part = p[:, lane : lane + HD]
                total = part if total is None else total + part
            part = jnp.dot(p.astype(jnp.bfloat16), v_held[j + o, c], preferred_element_type=jnp.float32)
            mixture = part if mixture is None else mixture + part
        if first:
            peak_kept[j, c] = jnp.broadcast_to(peak, mixture.shape)
            total_kept[j, c] = total
            mixture_kept[j, c] = mixture
            return None
        total = jnp.sum(total, axis=1, keepdims=True)
        return (mixture / total).astype(jnp.bfloat16)

    third = half // 3

    def project(part, cols):
        total = None
        for a in (part * third * HD, (half + part * third) * HD):
            b = a + third * HD
            product = jnp.dot(done[:, a:b], w_held[a:b, cols], preferred_element_type=jnp.float32)
            total = product if total is None else total + product
        return total

    def returned(part):
        for e in range(part * third, (part + 1) * third):
            back(e).wait_recv()

    def forward(c):
        for copy in from_pair(c)[:2]:
            copy.wait_recv()
        to_pair(c)[2].start()

        @pl.when(has_up)
        def _():
            for copy in pass_on(c, 0):
                copy.start()

        @pl.when(has_down)
        def _():
            for copy in pass_on(c, 1):
                copy.start()

    for c in range(AHEAD):
        forward(c)

    @pl.loop(0, half)
    def _(c):
        @pl.when(c + AHEAD < half)
        def _():
            forward(c + AHEAD)

        @pl.when(c < PIECES)
        def _():
            for k in range(1, chips):
                w_chip(k, c).start()
            w_sibling(0, c).start()

        own_in(c)[0].wait()

        @pl.when(has_down)
        def _():
            for copy in own_out(c, 0):
                copy.wait_recv()

        @pl.when(has_up)
        def _():
            for copy in own_out(c, 1):
                copy.wait_recv()

        attend(c, side, [0, 2 - side, 3 - side, 4], True)

    vis_got.wait_recv()

    @pl.loop(0, half)
    def _(c):
        from_pair(c)[2].wait_recv()
        attend(c, 1 - side, [1, 2, 3], True)

    @pl.loop(0, half)
    def _(c):
        @pl.when(c < PIECES)
        def _():
            for k in range(1, chips):
                w_chip(k, c).wait_recv()
                w_sibling(k, c).start()

        @pl.when(c == half - third)
        def _():
            w_in.wait()
            for k in range(chips):
                for i in range(PIECES):
                    w_sibling(k, i).wait()
                    if k > 0:
                        w_chip(k, i).wait_send()
            vis_out.wait_send()
            returned(0)

            @pl.loop(0, out_ref.shape[2] // BLOCK)
            def _(n):
                cols = pl.ds(pl.multiple_of(n * BLOCK, BLOCK), BLOCK)
                partial[:, cols] = project(0, cols)

        @pl.when(has_down)
        def _():
            for copy in pass_on(c, 0):
                copy.wait_recv()

        @pl.when(has_up)
        def _():
            for copy in pass_on(c, 1):
                copy.wait_recv()

        stage[c] = attend(c, 1 - side, [0, 4], False)
        back(c).start()
        head(side, c)[...] = attend(c, side, [1 + 2 * side], False)

        for copy in to_pair(c):
            copy.wait_send()

        @pl.when(has_up)
        def _():
            for copy in own_out(c, 0):
                copy.wait_send()

        @pl.when(has_down)
        def _():
            for copy in own_out(c, 1):
                copy.wait_send()

        @pl.when(has_up & (c > 0))
        def _():
            for copy in pass_on(c - 1, 0):
                copy.wait_send()

        @pl.when(has_down & (c > 0))
        def _():
            for copy in pass_on(c - 1, 1):
                copy.wait_send()

        @pl.when(c > 0)
        def _():
            back(c - 1).wait_send()

    returned(1)

    @pl.loop(0, out_ref.shape[2] // BLOCK)
    def _(n):
        cols = pl.ds(pl.multiple_of(n * BLOCK, BLOCK), BLOCK)
        partial[:, cols] += project(1, cols)

    returned(2)

    @pl.loop(0, out_ref.shape[2] // BLOCK)
    def _(n):
        cols = pl.ds(pl.multiple_of(n * BLOCK, BLOCK), BLOCK)
        out_ref[0, :, cols] = (partial[:, cols] + project(2, cols)).astype(jnp.bfloat16)

    @pl.when(has_up)
    def _():
        for copy in pass_on(half - 1, 0):
            copy.wait_send()

    @pl.when(has_down)
    def _():
        for copy in pass_on(half - 1, 1):
            copy.wait_send()

    back(half - 1).wait_send()


def per_device(queries, key_rows, value_rows, tile_lists, tile_counts, out_weight):
    tok_rows, channels = queries.shape[1], queries.shape[2]
    tiles = lax.axis_size("ctx")
    heads = channels // HD
    half = heads // 2
    hbm_spec = pl.BlockSpec(memory_space=pltpu.HBM)
    held = pltpu.VMEM((WINDOW, half, tok_rows, HD), jnp.bfloat16)
    kept = pltpu.VMEM((2, half, tok_rows, HD), jnp.float32)
    dma = pltpu.SemaphoreType.DMA
    pairs = 2 * tok_rows * SLOTS * tok_rows * half
    shards = lax.axis_size("dp")
    chips = shards // 2
    return pl.pallas_call(
        functools.partial(kernel, tiles, shards),
        out_shape=pltpu.VMEM((1, tok_rows, out_weight.shape[1]), jnp.bfloat16),
        in_specs=[hbm_spec] * 6,
        out_specs=pl.BlockSpec(memory_space=pltpu.VMEM),
        scratch_shapes=[
            pltpu.VMEM(tile_lists.shape, jnp.int32),
            pltpu.VMEM(tile_counts.shape, jnp.int32),
            pltpu.VMEM((8, HD), jnp.float32),
            pltpu.VMEM((2, half, tok_rows, HD), jnp.bfloat16),
            held,
            held,
            pltpu.VMEM((2, 8, HD), jnp.float32),
            pltpu.VMEM((tok_rows, channels), jnp.bfloat16),
            pltpu.VMEM((half, tok_rows, HD), jnp.bfloat16),
            pltpu.VMEM((channels, out_weight.shape[1]), jnp.bfloat16),
            kept,
            kept,
            kept,
            pltpu.VMEM((tok_rows, out_weight.shape[1]), jnp.float32),
            dma((1,)),
            dma((chips, PIECES)),
            dma((chips, PIECES)),
            dma((chips, PIECES)),
            dma((chips, PIECES)),
            dma((3, half)),
            dma((4,)),
            dma((3, half)),
            dma((3, half)),
            dma((2, 2, half)),
            dma((2, 2, half)),
            dma((2, 2, 2, half)),
            dma((half,)),
            dma((half,)),
        ],
        compiler_params=pltpu.CompilerParams(
            collective_id=0, has_side_effects=True, vmem_limit_bytes=60 * 1024 * 1024
        ),
        cost_estimate=pl.CostEstimate(
            flops=4 * pairs * HD, bytes_accessed=60_000_000, transcendentals=pairs
        ),
    )(queries, key_rows, value_rows, tile_lists, tile_counts, out_weight)


def solution(mesh):
    in_specs = (
        P("dp", "ctx", None),
        P("dp", "ctx", None),
        P("dp", "ctx", None),
        P("dp", "ctx", None),
        P("dp", "ctx"),
        P("dp", None),
    )
    out_specs = P("dp", "ctx", None)
    return jax.shard_map(
        per_device, mesh=mesh, in_specs=in_specs, out_specs=out_specs, check_vma=False
    )
```

```python
import functools
import math

import jax
import jax.numpy as jnp
from jax import lax
from jax.experimental import pallas as pl
from jax.experimental.pallas import tpu as pltpu
from jax.sharding import PartitionSpec as P

HD = 128
REACH = 2
SLOTS = 5
WINDOW = 6
HIDDEN = -1e30
SHUT = 1e30
BLOCK = 512
PIECES = 3
AHEAD = 2


def kernel(tiles, shards, q_ref, k_ref, v_ref, lists_ref, counts_ref, w_ref, out_ref,
           lists_held, counts_held, vis_mine, q_held, k_held, v_held, vis_held, done, stage, w_held, peak_kept, total_kept, mixture_kept, partial,
           w_own, w_send, w_recv, w_pass, w_core, own_sem, vis_sem, pair_send, pair_recv, own_send, pass_send, z_recv, back_send, back_recv):
    half = q_held.shape[1]
    me = lax.axis_index("ctx")
    row = lax.axis_index("dp")
    sibling = row + 1 - 2 * lax.rem(row, 2)
    depth = w_ref.shape[0]
    chips = shards // 2
    side = lax.rem(me, 2)
    pair = me + 1 - 2 * side
    has_up = me + 2 < tiles
    has_down = me >= 2
    up, down = me + 2, me - 2
    scale = math.log2(math.e) / math.sqrt(HD)

    def columns(ref, which, c):
        return ref.at[0, :, pl.ds(pl.multiple_of((which * half + c) * HD, HD), HD)]

    def remote(src, dst, send, recv, target):
        return pltpu.make_async_remote_copy(
            src_ref=src, dst_ref=dst, send_sem=send, recv_sem=recv,
            device_id={"ctx": target}, device_id_type=pl.DeviceIdType.MESH,
        )

    def to_pair(c):
        return [
            remote(columns(k_ref, 1 - side, c), k_held.at[2 + side, c], pair_send.at[0, c], pair_recv.at[0, c], pair),
            remote(columns(v_ref, 1 - side, c), v_held.at[2 + side, c], pair_send.at[1, c], pair_recv.at[1, c], pair),
            remote(columns(q_ref, 1 - side, c), q_held.at[side, c], pair_send.at[2, c], pair_recv.at[2, c], pair),
        ]

    def from_pair(c):
        other = 1 - side
        return [
            remote(columns(k_ref, side, c), k_held.at[2 + other, c], pair_send.at[0, c], pair_recv.at[0, c], pair),
            remote(columns(v_ref, side, c), v_held.at[2 + other, c], pair_send.at[1, c], pair_recv.at[1, c], pair),
            remote(columns(q_ref, side, c), q_held.at[other, c], pair_send.at[2, c], pair_recv.at[2, c], pair),
        ]

    def own_out(c, way):
        first, target = ((0, up), (4, down))[way]
        return [
            remote(k_held.at[2 + side, c], k_held.at[first + side, c], own_send.at[way, 0, c], z_recv.at[way, 0, 0, c], target),
            remote(v_held.at[2 + side, c], v_held.at[first + side, c], own_send.at[way, 1, c], z_recv.at[way, 0, 1, c], target),
        ]

    def pass_on(c, way):
        first, target = ((0, up), (4, down))[way]
        other = 1 - side
        return [
            remote(k_held.at[2 + other, c], k_held.at[first + other, c], pass_send.at[way, 0, c], z_recv.at[way, 1, 0, c], target),
            remote(v_held.at[2 + other, c], v_held.at[first + other, c], pass_send.at[way, 1, c], z_recv.at[way, 1, 1, c], target),
        ]

    def own_in(c):
        return [
            pltpu.make_async_copy(columns(q_ref, side, c), q_held.at[side, c], own_sem.at[0, c]),
            pltpu.make_async_copy(columns(k_ref, side, c), k_held.at[2 + side, c], own_sem.at[1, c]),
            pltpu.make_async_copy(columns(v_ref, side, c), v_held.at[2 + side, c], own_sem.at[2, c]),
        ]

    def head(which, c):
        return done.at[:, pl.ds(pl.multiple_of((which * half + c) * HD, HD), HD)]

    def back(c):
        return remote(stage.at[c], head(side, c), back_send.at[c], back_recv.at[c], pair)

    slab = depth // PIECES

    def shard(owner, i):
        return w_held.at[pl.ds(pl.multiple_of(owner * depth + i * slab, slab), slab)]

    def mine(i):
        return w_ref.at[pl.ds(pl.multiple_of(i * slab, slab), slab)]

    def w_copy(src, owner, i, send, recv, target):
        return pltpu.make_async_remote_copy(
            src_ref=src, dst_ref=shard(owner, i), send_sem=send, recv_sem=recv,
            device_id={"dp": target}, device_id_type=pl.DeviceIdType.MESH,
        )

    def w_chip(k, i):
        return w_copy(mine(i), row, i, w_send.at[k, i], w_recv.at[k, i], lax.rem(row + 2 * k, shards))

    def w_from(k):
        return lax.rem(row + shards - 2 * k, shards)

    def w_sibling(k, i):
        src = mine(i) if k == 0 else shard(w_from(k), i)
        return w_copy(src, w_from(k), i, w_pass.at[k, i], w_core.at[k, i], sibling)

    w_in = pltpu.make_async_copy(w_ref, w_held.at[pl.ds(pl.multiple_of(row * depth, depth), depth)], w_own.at[0])

    lists_in = pltpu.make_async_copy(lists_ref, lists_held, vis_sem.at[0])
    counts_in = pltpu.make_async_copy(counts_ref, counts_held, vis_sem.at[3])
    vis_out = remote(vis_mine, vis_held.at[side], vis_sem.at[1], vis_sem.at[2], pair)
    vis_got = remote(vis_mine, vis_held.at[1 - side], vis_sem.at[1], vis_sem.at[2], pair)

    barrier = pltpu.get_barrier_semaphore()

    def greet(target):
        pl.semaphore_signal(barrier, inc=1, device_id={"ctx": target}, device_id_type=pl.DeviceIdType.MESH)

    def greet_row(target):
        pl.semaphore_signal(barrier, inc=1, device_id={"dp": target}, device_id_type=pl.DeviceIdType.MESH)

    greet(pair)
    greet_row(sibling)
    for k in range(1, chips):
        greet_row(lax.rem(row + 2 * k, shards))

    @pl.when(has_up)
    def _():
        greet(up)

    @pl.when(has_down)
    def _():
        greet(down)

    lists_in.start()
    counts_in.start()

    @pl.loop(0, half)
    def _(c):
        for copy in own_in(c):
            copy.start()

    pl.semaphore_wait(barrier, 1 + chips + has_up.astype(jnp.int32) + has_down.astype(jnp.int32))

    @pl.loop(0, half)
    def _(c):
        for copy in to_pair(c)[:2]:
            copy.start()
        for copy in own_in(c)[1:]:
            copy.wait()

        @pl.when(has_up)
        def _():
            for copy in own_out(c, 0):
                copy.start()

        @pl.when(has_down)
        def _():
            for copy in own_out(c, 1):
                copy.start()

    w_in.start()

    lists_in.wait()
    counts_in.wait()
    listed = lists_held[0]
    live = lax.broadcasted_iota(jnp.int32, listed.shape, 1) < counts_held[...]
    for o in range(SLOTS):
        match = jnp.where((listed == me + (o - REACH)) & live, 1.0, 0.0)
        row_seen = jnp.max(match, axis=1, keepdims=True)
        vis_mine[o : o + 1, :] = jnp.broadcast_to(row_seen, (1, HD))
        vis_held[side, o : o + 1, :] = jnp.broadcast_to(row_seen, (1, HD))
    vis_out.start()

    @pl.when(jnp.logical_not(has_down))
    def _():
        k_held[0:2] = jnp.zeros((2,) + k_held.shape[1:], k_held.dtype)
        v_held[0:2] = jnp.zeros((2,) + v_held.shape[1:], v_held.dtype)

    @pl.when(jnp.logical_not(has_up))
    def _():
        k_held[4:6] = jnp.zeros((2,) + k_held.shape[1:], k_held.dtype)
        v_held[4:6] = jnp.zeros((2,) + v_held.shape[1:], v_held.dtype)

    def attend(c, j, offsets, first):
        q = q_held[j, c]
        seen = [vis_held[j, pl.ds(o, 1), :] > 0.0 for o in offsets]
        keys = jnp.concatenate([k_held[j + o, c] for o in offsets], axis=0)
        values = jnp.concatenate([v_held[j + o, c] for o in offsets], axis=0)
        every = lax.dot_general(q, keys, (((1,), (1,)), ((), ())), preferred_element_type=jnp.float32)
        wide = k_held.shape[2]
        scores = [every[:, i * wide : (i + 1) * wide] for i in range(len(offsets))]
        peak = None
        for see, s in zip(seen, scores):
            top = s[:, :HD]
            for lane in range(HD, s.shape[1], HD):
                top = jnp.maximum(top, s[:, lane : lane + HD])
            top = jnp.where(see, top, HIDDEN)
            peak = top if peak is None else jnp.maximum(peak, top)
        peak = jnp.max(peak, axis=1, keepdims=True) * scale
        if first:
            total, mixture = None, None
        else:
            before = peak_kept[j, c][:, :1]
            peak = jnp.maximum(peak, before)
            fade = jnp.exp2(before - peak)
            total, mixture = total_kept[j, c] * fade, mixture_kept[j, c] * fade
        probs = []
        for see, s in zip(seen, scores):
            shift = jnp.where(see[:, :1], peak, SHUT)
            p = jnp.exp2(s * scale - shift)
            for lane in range(0, p.shape[1], HD):
                part = p[:, lane : lane + HD]
                total = part if total is None else total + part
            probs.append(p.astype(jnp.bfloat16))
        product = jnp.dot(jnp.concatenate(probs, axis=1), values, preferred_element_type=jnp.float32)
        mixture = product if mixture is None else mixture + product
        if first:
            peak_kept[j, c] = jnp.broadcast_to(peak, mixture.shape)
            total_kept[j, c] = total
            mixture_kept[j, c] = mixture
            return None
        total = jnp.sum(total, axis=1, keepdims=True)
        return (mixture / total).astype(jnp.bfloat16)

    third = half // 3

    def project(part, cols):
        starts = (part * third * HD, (half + part * third) * HD)
        left = jnp.concatenate([done[:, a : a + third * HD] for a in starts], axis=1)
        right = jnp.concatenate([w_held[a : a + third * HD, cols] for a in starts], axis=0)
        return jnp.dot(left, right, preferred_element_type=jnp.float32)

    def returned(part):
        for e in range(part * third, (part + 1) * third):
            back(e).wait_recv()

    def forward(c):
        for copy in from_pair(c)[:2]:
            copy.wait_recv()
        to_pair(c)[2].start()

        @pl.when(has_up)
        def _():
            for copy in pass_on(c, 0):
                copy.start()

        @pl.when(has_down)
        def _():
            for copy in pass_on(c, 1):
                copy.start()

    for c in range(AHEAD):
        forward(c)

    @pl.loop(0, half)
    def _(c):
        @pl.when(c + AHEAD < half)
        def _():
            forward(c + AHEAD)

        @pl.when(c < PIECES)
        def _():
            for k in range(1, chips):
                w_chip(k, c).start()
            w_sibling(0, c).start()

        own_in(c)[0].wait()

        @pl.when(has_down)
        def _():
            for copy in own_out(c, 0):
                copy.wait_recv()

        @pl.when(has_up)
        def _():
            for copy in own_out(c, 1):
                copy.wait_recv()

        attend(c, side, [0, 2 - side, 3 - side, 4], True)

    vis_got.wait_recv()

    @pl.loop(0, half)
    def _(c):
        from_pair(c)[2].wait_recv()
        attend(c, 1 - side, [1, 2, 3], True)

    @pl.loop(0, half)
    def _(c):
        @pl.when(c < PIECES)
        def _():
            for k in range(1, chips):
                w_chip(k, c).wait_recv()
                w_sibling(k, c).start()

        @pl.when(c == half - third)
        def _():
            w_in.wait()
            for k in range(chips):
                for i in range(PIECES):
                    w_sibling(k, i).wait()
                    if k > 0:
                        w_chip(k, i).wait_send()
            vis_out.wait_send()
            returned(0)

            @pl.loop(0, out_ref.shape[2] // BLOCK)
            def _(n):
                cols = pl.ds(pl.multiple_of(n * BLOCK, BLOCK), BLOCK)
                partial[:, cols] = project(0, cols)

        @pl.when(has_down)
        def _():
            for copy in pass_on(c, 0):
                copy.wait_recv()

        @pl.when(has_up)
        def _():
            for copy in pass_on(c, 1):
                copy.wait_recv()

        stage[c] = attend(c, 1 - side, [0, 4], False)
        back(c).start()
        head(side, c)[...] = attend(c, side, [1 + 2 * side], False)

        for copy in to_pair(c):
            copy.wait_send()

        @pl.when(has_up)
        def _():
            for copy in own_out(c, 0):
                copy.wait_send()

        @pl.when(has_down)
        def _():
            for copy in own_out(c, 1):
                copy.wait_send()

        @pl.when(has_up & (c > 0))
        def _():
            for copy in pass_on(c - 1, 0):
                copy.wait_send()

        @pl.when(has_down & (c > 0))
        def _():
            for copy in pass_on(c - 1, 1):
                copy.wait_send()

        @pl.when(c > 0)
        def _():
            back(c - 1).wait_send()

    returned(1)

    @pl.loop(0, out_ref.shape[2] // BLOCK)
    def _(n):
        cols = pl.ds(pl.multiple_of(n * BLOCK, BLOCK), BLOCK)
        partial[:, cols] += project(1, cols)

    returned(2)

    @pl.loop(0, out_ref.shape[2] // BLOCK)
    def _(n):
        cols = pl.ds(pl.multiple_of(n * BLOCK, BLOCK), BLOCK)
        out_ref[0, :, cols] = (partial[:, cols] + project(2, cols)).astype(jnp.bfloat16)

    @pl.when(has_up)
    def _():
        for copy in pass_on(half - 1, 0):
            copy.wait_send()

    @pl.when(has_down)
    def _():
        for copy in pass_on(half - 1, 1):
            copy.wait_send()

    back(half - 1).wait_send()


def per_device(queries, key_rows, value_rows, tile_lists, tile_counts, out_weight):
    tok_rows, channels = queries.shape[1], queries.shape[2]
    tiles = lax.axis_size("ctx")
    heads = channels // HD
    half = heads // 2
    hbm_spec = pl.BlockSpec(memory_space=pltpu.HBM)
    held = pltpu.VMEM((WINDOW, half, tok_rows, HD), jnp.bfloat16)
    kept = pltpu.VMEM((2, half, tok_rows, HD), jnp.float32)
    dma = pltpu.SemaphoreType.DMA
    pairs = 2 * tok_rows * SLOTS * tok_rows * half
    shards = lax.axis_size("dp")
    chips = shards // 2
    return pl.pallas_call(
        functools.partial(kernel, tiles, shards),
        out_shape=pltpu.VMEM((1, tok_rows, out_weight.shape[1]), jnp.bfloat16),
        in_specs=[hbm_spec] * 6,
        out_specs=pl.BlockSpec(memory_space=pltpu.VMEM),
        scratch_shapes=[
            pltpu.VMEM(tile_lists.shape, jnp.int32),
            pltpu.VMEM(tile_counts.shape, jnp.int32),
            pltpu.VMEM((8, HD), jnp.float32),
            pltpu.VMEM((2, half, tok_rows, HD), jnp.bfloat16),
            held,
            held,
            pltpu.VMEM((2, 8, HD), jnp.float32),
            pltpu.VMEM((tok_rows, channels), jnp.bfloat16),
            pltpu.VMEM((half, tok_rows, HD), jnp.bfloat16),
            pltpu.VMEM((channels, out_weight.shape[1]), jnp.bfloat16),
            kept,
            kept,
            kept,
            pltpu.VMEM((tok_rows, out_weight.shape[1]), jnp.float32),
            dma((1,)),
            dma((chips, PIECES)),
            dma((chips, PIECES)),
            dma((chips, PIECES)),
            dma((chips, PIECES)),
            dma((3, half)),
            dma((4,)),
            dma((3, half)),
            dma((3, half)),
            dma((2, 2, half)),
            dma((2, 2, half)),
            dma((2, 2, 2, half)),
            dma((half,)),
            dma((half,)),
        ],
        compiler_params=pltpu.CompilerParams(
            collective_id=0, has_side_effects=True, vmem_limit_bytes=60 * 1024 * 1024
        ),
        cost_estimate=pl.CostEstimate(
            flops=4 * pairs * HD, bytes_accessed=60_000_000, transcendentals=pairs
        ),
    )(queries, key_rows, value_rows, tile_lists, tile_counts, out_weight)


def solution(mesh):
    in_specs = (
        P("dp", "ctx", None),
        P("dp", "ctx", None),
        P("dp", "ctx", None),
        P("dp", "ctx", None),
        P("dp", "ctx"),
        P("dp", None),
    )
    out_specs = P("dp", "ctx", None)
    return jax.shard_map(
        per_device, mesh=mesh, in_specs=in_specs, out_specs=out_specs, check_vma=False
    )
```

```python
import functools
import math

import jax
import jax.numpy as jnp
from jax import lax
from jax.experimental import pallas as pl
from jax.experimental.pallas import tpu as pltpu
from jax.sharding import PartitionSpec as P

HD = 128
REACH = 2
SLOTS = 5
WINDOW = 6
HIDDEN = -1e30
SHUT = 1e30
BLOCK = 512
PIECES = 3
AHEAD = 3


def kernel(tiles, shards, q_ref, k_ref, v_ref, lists_ref, counts_ref, w_ref, out_ref,
           lists_held, counts_held, vis_mine, q_held, k_held, v_held, vis_held, done, stage, w_held, peak_kept, total_kept, mixture_kept, partial,
           w_own, w_send, w_recv, w_pass, w_core, own_sem, vis_sem, pair_send, pair_recv, own_send, pass_send, z_recv, back_send, back_recv):
    half = q_held.shape[1]
    me = lax.axis_index("ctx")
    row = lax.axis_index("dp")
    sibling = row + 1 - 2 * lax.rem(row, 2)
    depth = w_ref.shape[0]
    chips = shards // 2
    side = lax.rem(me, 2)
    pair = me + 1 - 2 * side
    has_up = me + 2 < tiles
    has_down = me >= 2
    up, down = me + 2, me - 2
    scale = math.log2(math.e) / math.sqrt(HD)

    def columns(ref, which, c):
        return ref.at[0, :, pl.ds(pl.multiple_of((which * half + c) * HD, HD), HD)]

    def remote(src, dst, send, recv, target):
        return pltpu.make_async_remote_copy(
            src_ref=src, dst_ref=dst, send_sem=send, recv_sem=recv,
            device_id={"ctx": target}, device_id_type=pl.DeviceIdType.MESH,
        )

    def to_pair(c):
        return [
            remote(columns(k_ref, 1 - side, c), k_held.at[2 + side, c], pair_send.at[0, c], pair_recv.at[0, c], pair),
            remote(columns(v_ref, 1 - side, c), v_held.at[2 + side, c], pair_send.at[1, c], pair_recv.at[1, c], pair),
            remote(columns(q_ref, 1 - side, c), q_held.at[side, c], pair_send.at[2, c], pair_recv.at[2, c], pair),
        ]

    def from_pair(c):
        other = 1 - side
        return [
            remote(columns(k_ref, side, c), k_held.at[2 + other, c], pair_send.at[0, c], pair_recv.at[0, c], pair),
            remote(columns(v_ref, side, c), v_held.at[2 + other, c], pair_send.at[1, c], pair_recv.at[1, c], pair),
            remote(columns(q_ref, side, c), q_held.at[other, c], pair_send.at[2, c], pair_recv.at[2, c], pair),
        ]

    def own_out(c, way):
        first, target = ((0, up), (4, down))[way]
        return [
            remote(k_held.at[2 + side, c], k_held.at[first + side, c], own_send.at[way, 0, c], z_recv.at[way, 0, 0, c], target),
            remote(v_held.at[2 + side, c], v_held.at[first + side, c], own_send.at[way, 1, c], z_recv.at[way, 0, 1, c], target),
        ]

    def pass_on(c, way):
        first, target = ((0, up), (4, down))[way]
        other = 1 - side
        return [
            remote(k_held.at[2 + other, c], k_held.at[first + other, c], pass_send.at[way, 0, c], z_recv.at[way, 1, 0, c], target),
            remote(v_held.at[2 + other, c], v_held.at[first + other, c], pass_send.at[way, 1, c], z_recv.at[way, 1, 1, c], target),
        ]

    def own_in(c):
        return [
            pltpu.make_async_copy(columns(q_ref, side, c), q_held.at[side, c], own_sem.at[0, c]),
            pltpu.make_async_copy(columns(k_ref, side, c), k_held.at[2 + side, c], own_sem.at[1, c]),
            pltpu.make_async_copy(columns(v_ref, side, c), v_held.at[2 + side, c], own_sem.at[2, c]),
        ]

    def head(which, c):
        return done.at[:, pl.ds(pl.multiple_of((which * half + c) * HD, HD), HD)]

    def back(c):
        return remote(stage.at[c], head(side, c), back_send.at[c], back_recv.at[c], pair)

    slab = depth // PIECES

    def shard(owner, i):
        return w_held.at[pl.ds(pl.multiple_of(owner * depth + i * slab, slab), slab)]

    def mine(i):
        return w_ref.at[pl.ds(pl.multiple_of(i * slab, slab), slab)]

    def w_copy(src, owner, i, send, recv, target):
        return pltpu.make_async_remote_copy(
            src_ref=src, dst_ref=shard(owner, i), send_sem=send, recv_sem=recv,
            device_id={"dp": target}, device_id_type=pl.DeviceIdType.MESH,
        )

    def w_chip(k, i):
        return w_copy(mine(i), row, i, w_send.at[k, i], w_recv.at[k, i], lax.rem(row + 2 * k, shards))

    def w_from(k):
        return lax.rem(row + shards - 2 * k, shards)

    def w_sibling(k, i):
        src = mine(i) if k == 0 else shard(w_from(k), i)
        return w_copy(src, w_from(k), i, w_pass.at[k, i], w_core.at[k, i], sibling)

    w_in = pltpu.make_async_copy(w_ref, w_held.at[pl.ds(pl.multiple_of(row * depth, depth), depth)], w_own.at[0])

    lists_in = pltpu.make_async_copy(lists_ref, lists_held, vis_sem.at[0])
    counts_in = pltpu.make_async_copy(counts_ref, counts_held, vis_sem.at[3])
    vis_out = remote(vis_mine, vis_held.at[side], vis_sem.at[1], vis_sem.at[2], pair)
    vis_got = remote(vis_mine, vis_held.at[1 - side], vis_sem.at[1], vis_sem.at[2], pair)

    barrier = pltpu.get_barrier_semaphore()

    def greet(target):
        pl.semaphore_signal(barrier, inc=1, device_id={"ctx": target}, device_id_type=pl.DeviceIdType.MESH)

    def greet_row(target):
        pl.semaphore_signal(barrier, inc=1, device_id={"dp": target}, device_id_type=pl.DeviceIdType.MESH)

    greet(pair)
    greet_row(sibling)
    for k in range(1, chips):
        greet_row(lax.rem(row + 2 * k, shards))

    @pl.when(has_up)
    def _():
        greet(up)

    @pl.when(has_down)
    def _():
        greet(down)

    lists_in.start()
    counts_in.start()

    @pl.loop(0, half)
    def _(c):
        for copy in own_in(c):
            copy.start()

    pl.semaphore_wait(barrier, 1 + chips + has_up.astype(jnp.int32) + has_down.astype(jnp.int32))

    @pl.loop(0, half)
    def _(c):
        for copy in to_pair(c)[:2]:
            copy.start()
        for copy in own_in(c)[1:]:
            copy.wait()

        @pl.when(has_up)
        def _():
            for copy in own_out(c, 0):
                copy.start()

        @pl.when(has_down)
        def _():
            for copy in own_out(c, 1):
                copy.start()

    w_in.start()

    lists_in.wait()
    counts_in.wait()
    listed = lists_held[0]
    live = lax.broadcasted_iota(jnp.int32, listed.shape, 1) < counts_held[...]
    for o in range(SLOTS):
        match = jnp.where((listed == me + (o - REACH)) & live, 1.0, 0.0)
        row_seen = jnp.max(match, axis=1, keepdims=True)
        vis_mine[o : o + 1, :] = jnp.broadcast_to(row_seen, (1, HD))
        vis_held[side, o : o + 1, :] = jnp.broadcast_to(row_seen, (1, HD))
    vis_out.start()

    @pl.when(jnp.logical_not(has_down))
    def _():
        k_held[0:2] = jnp.zeros((2,) + k_held.shape[1:], k_held.dtype)
        v_held[0:2] = jnp.zeros((2,) + v_held.shape[1:], v_held.dtype)

    @pl.when(jnp.logical_not(has_up))
    def _():
        k_held[4:6] = jnp.zeros((2,) + k_held.shape[1:], k_held.dtype)
        v_held[4:6] = jnp.zeros((2,) + v_held.shape[1:], v_held.dtype)

    def attend(c, j, offsets, first):
        q = q_held[j, c]
        seen = [vis_held[j, pl.ds(o, 1), :] > 0.0 for o in offsets]
        keys = jnp.concatenate([k_held[j + o, c] for o in offsets], axis=0)
        values = jnp.concatenate([v_held[j + o, c] for o in offsets], axis=0)
        every = lax.dot_general(q, keys, (((1,), (1,)), ((), ())), preferred_element_type=jnp.float32)
        wide = k_held.shape[2]
        scores = [every[:, i * wide : (i + 1) * wide] for i in range(len(offsets))]
        peak = None
        for see, s in zip(seen, scores):
            top = s[:, :HD]
            for lane in range(HD, s.shape[1], HD):
                top = jnp.maximum(top, s[:, lane : lane + HD])
            top = jnp.where(see, top, HIDDEN)
            peak = top if peak is None else jnp.maximum(peak, top)
        peak = jnp.max(peak, axis=1, keepdims=True) * scale
        if first:
            total, mixture = None, None
        else:
            before = peak_kept[j, c][:, :1]
            peak = jnp.maximum(peak, before)
            fade = jnp.exp2(before - peak)
            total, mixture = total_kept[j, c] * fade, mixture_kept[j, c] * fade
        probs = []
        for see, s in zip(seen, scores):
            shift = jnp.where(see[:, :1], peak, SHUT)
            p = jnp.exp2(s * scale - shift)
            for lane in range(0, p.shape[1], HD):
                part = p[:, lane : lane + HD]
                total = part if total is None else total + part
            probs.append(p.astype(jnp.bfloat16))
        product = jnp.dot(jnp.concatenate(probs, axis=1), values, preferred_element_type=jnp.float32)
        mixture = product if mixture is None else mixture + product
        if first:
            peak_kept[j, c] = jnp.broadcast_to(peak, mixture.shape)
            total_kept[j, c] = total
            mixture_kept[j, c] = mixture
            return None
        total = jnp.sum(total, axis=1, keepdims=True)
        return (mixture / total).astype(jnp.bfloat16)

    third = half // 3

    def project(part, cols):
        starts = (part * third * HD, (half + part * third) * HD)
        left = jnp.concatenate([done[:, a : a + third * HD] for a in starts], axis=1)
        right = jnp.concatenate([w_held[a : a + third * HD, cols] for a in starts], axis=0)
        return jnp.dot(left, right, preferred_element_type=jnp.float32)

    def returned(part):
        for e in range(part * third, (part + 1) * third):
            back(e).wait_recv()

    def forward(c):
        for copy in from_pair(c)[:2]:
            copy.wait_recv()
        to_pair(c)[2].start()

        @pl.when(has_up)
        def _():
            for copy in pass_on(c, 0):
                copy.start()

        @pl.when(has_down)
        def _():
            for copy in pass_on(c, 1):
                copy.start()

    for c in range(AHEAD):
        forward(c)

    @pl.loop(0, half)
    def _(c):
        @pl.when(c + AHEAD < half)
        def _():
            forward(c + AHEAD)

        @pl.when(c < PIECES)
        def _():
            for k in range(1, chips):
                w_chip(k, c).start()
            w_sibling(0, c).start()

        own_in(c)[0].wait()

        @pl.when(has_down)
        def _():
            for copy in own_out(c, 0):
                copy.wait_recv()

        @pl.when(has_up)
        def _():
            for copy in own_out(c, 1):
                copy.wait_recv()

        attend(c, side, [0, 2 - side, 3 - side, 4], True)

    vis_got.wait_recv()

    @pl.loop(0, half)
    def _(c):
        from_pair(c)[2].wait_recv()
        attend(c, 1 - side, [1, 2, 3], True)

    @pl.loop(0, half)
    def _(c):
        @pl.when(c < PIECES)
        def _():
            for k in range(1, chips):
                w_chip(k, c).wait_recv()
                w_sibling(k, c).start()

        @pl.when(c == half - third)
        def _():
            w_in.wait()
            for k in range(chips):
                for i in range(PIECES):
                    w_sibling(k, i).wait()
                    if k > 0:
                        w_chip(k, i).wait_send()
            vis_out.wait_send()
            returned(0)

            @pl.loop(0, out_ref.shape[2] // BLOCK)
            def _(n):
                cols = pl.ds(pl.multiple_of(n * BLOCK, BLOCK), BLOCK)
                partial[:, cols] = project(0, cols)

        @pl.when(has_down)
        def _():
            for copy in pass_on(c, 0):
                copy.wait_recv()

        @pl.when(has_up)
        def _():
            for copy in pass_on(c, 1):
                copy.wait_recv()

        stage[c] = attend(c, 1 - side, [0, 4], False)
        back(c).start()
        head(side, c)[...] = attend(c, side, [1 + 2 * side], False)

        for copy in to_pair(c):
            copy.wait_send()

        @pl.when(has_up)
        def _():
            for copy in own_out(c, 0):
                copy.wait_send()

        @pl.when(has_down)
        def _():
            for copy in own_out(c, 1):
                copy.wait_send()

        @pl.when(has_up & (c > 0))
        def _():
            for copy in pass_on(c - 1, 0):
                copy.wait_send()

        @pl.when(has_down & (c > 0))
        def _():
            for copy in pass_on(c - 1, 1):
                copy.wait_send()

        @pl.when(c > 0)
        def _():
            back(c - 1).wait_send()

    returned(1)

    @pl.loop(0, out_ref.shape[2] // BLOCK)
    def _(n):
        cols = pl.ds(pl.multiple_of(n * BLOCK, BLOCK), BLOCK)
        partial[:, cols] += project(1, cols)

    returned(2)

    @pl.loop(0, out_ref.shape[2] // BLOCK)
    def _(n):
        cols = pl.ds(pl.multiple_of(n * BLOCK, BLOCK), BLOCK)
        out_ref[0, :, cols] = (partial[:, cols] + project(2, cols)).astype(jnp.bfloat16)

    @pl.when(has_up)
    def _():
        for copy in pass_on(half - 1, 0):
            copy.wait_send()

    @pl.when(has_down)
    def _():
        for copy in pass_on(half - 1, 1):
            copy.wait_send()

    back(half - 1).wait_send()


def per_device(queries, key_rows, value_rows, tile_lists, tile_counts, out_weight):
    tok_rows, channels = queries.shape[1], queries.shape[2]
    tiles = lax.axis_size("ctx")
    heads = channels // HD
    half = heads // 2
    hbm_spec = pl.BlockSpec(memory_space=pltpu.HBM)
    held = pltpu.VMEM((WINDOW, half, tok_rows, HD), jnp.bfloat16)
    kept = pltpu.VMEM((2, half, tok_rows, HD), jnp.float32)
    dma = pltpu.SemaphoreType.DMA
    pairs = 2 * tok_rows * SLOTS * tok_rows * half
    shards = lax.axis_size("dp")
    chips = shards // 2
    return pl.pallas_call(
        functools.partial(kernel, tiles, shards),
        out_shape=pltpu.VMEM((1, tok_rows, out_weight.shape[1]), jnp.bfloat16),
        in_specs=[hbm_spec] * 6,
        out_specs=pl.BlockSpec(memory_space=pltpu.VMEM),
        scratch_shapes=[
            pltpu.VMEM(tile_lists.shape, jnp.int32),
            pltpu.VMEM(tile_counts.shape, jnp.int32),
            pltpu.VMEM((8, HD), jnp.float32),
            pltpu.VMEM((2, half, tok_rows, HD), jnp.bfloat16),
            held,
            held,
            pltpu.VMEM((2, 8, HD), jnp.float32),
            pltpu.VMEM((tok_rows, channels), jnp.bfloat16),
            pltpu.VMEM((half, tok_rows, HD), jnp.bfloat16),
            pltpu.VMEM((channels, out_weight.shape[1]), jnp.bfloat16),
            kept,
            kept,
            kept,
            pltpu.VMEM((tok_rows, out_weight.shape[1]), jnp.float32),
            dma((1,)),
            dma((chips, PIECES)),
            dma((chips, PIECES)),
            dma((chips, PIECES)),
            dma((chips, PIECES)),
            dma((3, half)),
            dma((4,)),
            dma((3, half)),
            dma((3, half)),
            dma((2, 2, half)),
            dma((2, 2, half)),
            dma((2, 2, 2, half)),
            dma((half,)),
            dma((half,)),
        ],
        compiler_params=pltpu.CompilerParams(
            collective_id=0, has_side_effects=True, vmem_limit_bytes=60 * 1024 * 1024
        ),
        cost_estimate=pl.CostEstimate(
            flops=4 * pairs * HD, bytes_accessed=60_000_000, transcendentals=pairs
        ),
    )(queries, key_rows, value_rows, tile_lists, tile_counts, out_weight)


def solution(mesh):
    in_specs = (
        P("dp", "ctx", None),
        P("dp", "ctx", None),
        P("dp", "ctx", None),
        P("dp", "ctx", None),
        P("dp", "ctx"),
        P("dp", None),
    )
    out_specs = P("dp", "ctx", None)
    return jax.shard_map(
        per_device, mesh=mesh, in_specs=in_specs, out_specs=out_specs, check_vma=False
    )
```
